32 devices in a mesh: rep: 4 (over z), grp: 8 (over y, x, core).
Axes of the slice: x: 2, y: 2, z: 4, core: 2. Of those that a mesh axis runs over, the one named last changes fastest.
Arguments:
- tokens: bfloat16 [16384, 1792], P(('rep', 'grp')), may hold values from -6 to 6
- seg_ids: int32 [16384], P(('rep', 'grp')), may hold values from 0 to 16383, as said below
- valid_mask: int32 [16384], P(('rep', 'grp')), may hold values 0 or 1
- norm_gain: float32 [1792], replicated, may hold values from 0.5 to 1.5
- conv_taps: float32 [1792, 3], replicated, may hold values from -4 to 4
- mix_in: bfloat16 [1792, 2304], P('grp'), may hold values from -0.25 to 0.25
- mix_out: bfloat16 [1792, 1792], P('grp'), may hold values from -1 to 1
- ffn_gain: float32 [1792], replicated, may hold values from 0.5 to 1.5
- ffn_in: bfloat16 [3584, 3584], P('grp'), may hold values from -0.125 to 0.125
- ffn_out: bfloat16 [3584, 1792], P('grp'), may hold values from -0.09375 to 0.09375
- grad_out: bfloat16 [16384, 1792], P(('rep', 'grp')), may hold values from -6 to 6
Outputs:
- mixed_out: bfloat16 [16384, 1792], P(('rep', 'grp'))
- grad_tokens: bfloat16 [16384, 1792], P(('rep', 'grp'))
- grad_norm_gain: float32 [1792], replicated
- grad_conv_taps: float32 [1792, 3], replicated
- grad_mix_in: float32 [1792, 2304], P('grp')
- grad_mix_out: float32 [1792, 1792], P('grp')
- grad_ffn_gain: float32 [1792], replicated
- grad_ffn_in: float32 [3584, 3584], P('grp')
- grad_ffn_out: float32 [3584, 1792], P('grp')
- layer_stats: float32 [3], replicated
The draws below stay inside these ranges and needn't reach their ends.
Inputs may be any that keep to these rules, and one draw needn't show every extreme that they name: `seg_ids`: ids never fall; the first token of every block of 4096 tokens has a larger id than the token before it; the first token's id is 0 and the last token's id is 16383.
All inputs are finite; a program needn't handle non-finite values. No bound on the sum of `valid_mask` on one device may be relied on, other than what follows from the above.
Results may differ from the reference program's by a relative error of at most 0.018.
The reference program's roundings to bfloat16 on the way count: a program that leaves them out, or rounds other values in their place, can miss the bound.
Values may be sent and summed in bfloat16 or wider, within the bound.
No kernel may reach another device: no remote copies, remote signals or barrier semaphores. Data moves between devices by JAX's collectives and lax.ppermute only.
A program may use at most 448 MiB of HBM per device.

```python
import math
import jax
import jax.numpy as jnp
from jax import lax

D = 1792
HEADS = 16
FEAT = 16
VDIM = 112
FF = 3584
PHI = 273
TOK_DEV = 512
GROUP_TOKENS = 4096
TOKENS = 16384


def draw_seg_ids(key, part):
    key = jax.random.fold_in(key, 11)
    groups = TOKENS // GROUP_TOKENS
    begin_key, end_key, mark_key = jax.random.split(key, 3)
    starts = jax.random.randint(begin_key, (groups,), 1, TOK_DEV // 2 + 1)
    stops = GROUP_TOKENS - jax.random.randint(end_key, (groups,), 1, TOK_DEV // 2 + 1)
    position = jnp.arange(TOKENS, dtype=jnp.int32)
    local_pos = position % GROUP_TOKENS
    group_of = position // GROUP_TOKENS
    start_at = starts[group_of]
    stop_at = stops[group_of]
    random_marks = jax.random.randint(mark_key, (TOKENS,), 0, 16) == 0
    outside = (local_pos < start_at) | (local_pos > stop_at)
    marks = (local_pos == 0) | (local_pos == start_at) | (local_pos == stop_at) | outside & random_marks
    dense_ids = (jnp.cumsum(marks.astype(jnp.int32)) - 1).astype(jnp.int32)
    final_id = dense_ids[TOKENS - 1]
    return jnp.where(dense_ids == final_id, jnp.int32(TOKENS - 1), dense_ids).astype(jnp.int32)


def set_ends(values, own_key, least, top_value):
    spot = [jax.random.randint(jax.random.fold_in(own_key, axis), (), 0, length) for axis, length in enumerate(values.shape)]
    widest = values.shape.index(max(values.shape))
    beside = spot[:widest] + [(spot[widest] + 1) % values.shape[widest]] + spot[widest + 1:]
    return values.at[tuple(spot)].set(least).at[tuple(beside)].set(top_value)


def level_of(key, extent, shards, low, high):
    def one(dim, shards_of):
        heights = jax.random.uniform(jax.random.fold_in(jax.random.fold_in(key, 6), dim), (shards_of,), jnp.float32, low / len(shards), high / len(shards))
        return jnp.repeat(jnp.exp(heights), extent[dim] // shards_of).reshape((-1,) + (1,) * (len(extent) - dim - 1))

    gain = one(*shards[0])
    for cut in shards[1:]:
        gain = gain * one(*cut)
    return gain


def normal_values(key, shape, deviation, reach, cuts=(), kind=jnp.bfloat16):
    drawn = deviation * jax.random.normal(key, shape, jnp.float32)
    if cuts:
        drawn = drawn * level_of(key, shape, cuts, -0.22, 0.18)
    return jnp.clip(drawn, -reach, reach).astype(kind)


def setup_inputs(seed: int = 0) -> dict:
    key_list = jax.random.split(jax.random.key(seed), 12)
    return {
        "tokens": normal_values(key_list[0], (TOKENS, D), 1.0, 6.0, ((0, 32),)),
        "seg_ids": draw_seg_ids(jax.random.fold_in(key_list[11], 71), 0),
        "valid_mask": set_ends((jax.random.randint(key_list[2], (TOKENS,), 0, 8) < 7).astype(jnp.int32), jax.random.fold_in(key_list[2], 1), 0, 1),
        "norm_gain": jnp.clip(1.0 + 0.1 * jax.random.normal(key_list[3], (D,), jnp.float32), 0.5, 1.5),
        "conv_taps": normal_values(key_list[4], (D, 3), 0.7, 4.0, (), jnp.float32),
        "mix_in": normal_values(key_list[5], (D, 2 * HEADS * FEAT + HEADS * VDIM), (D // 4) ** -0.5, 0.25, ((0, 8),)),
        "mix_out": normal_values(key_list[6], (HEADS * VDIM, D), (D // 64) ** -0.5, 1.0, ((0, 8),)),
        "ffn_gain": jnp.clip(1.0 + 0.1 * jax.random.normal(key_list[7], (D,), jnp.float32), 0.5, 1.5),
        "ffn_in": normal_values(key_list[8], (FF, 2 * D), D ** -0.5, 0.125, ((0, 8),)),
        "ffn_out": normal_values(key_list[9], (FF, D), FF ** -0.5, 0.09375, ((0, 8),)),
        "grad_out": normal_values(key_list[10], (TOKENS, D), 1.0, 6.0, ((0, 32),)),
    }


EPSILON = 1e-05
HIGHEST = lax.Precision.HIGHEST
OUTER_SCALE = 0.25 / math.sqrt(2.0)

@jax.custom_vjp
def low(v):
    return lax.optimization_barrier(v.astype(jnp.bfloat16)).astype(jnp.float32)

@jax.custom_vjp
def low_back(v):
    return v

def low_keep(v):
    return (low(v), None)

def low_pass(kept, grad):
    return (grad,)

def back_keep(v):
    return (v, None)

def back_low(kept, grad):
    return (low(grad),)
low.defvjp(low_keep, low_pass)
low_back.defvjp(back_keep, back_low)

def feature_map(inputs):
    lead = inputs.shape[:-1]
    outer = (inputs[..., :, None] * inputs[..., None, :]).reshape(lead + (FEAT * FEAT,))
    return jnp.concatenate([jnp.ones_like(inputs[..., :1]), inputs * 0.5, outer * OUTER_SCALE], axis=-1)

def attend_block(running, pieces):
    states, totals, last_seen = running
    queries, keys_in, values, seg_rows, keep_rows = pieces
    row_count = seg_rows.shape[0]
    positions = jnp.arange(row_count)
    allowed = ((positions[:, None] >= positions[None, :]) & (seg_rows[:, None] == seg_rows[None, :])).astype(jnp.float32) * keep_rows[None, :]
    scores = low_back(jnp.einsum('thf,shf->hts', queries, keys_in, precision=HIGHEST) * 0.25)
    weights = (1.0 + scores + 0.5 * scores * scores) * allowed[None]
    local_num = jnp.einsum('hts,shv->thv', low(weights), values, precision=HIGHEST)
    local_den = lax.optimization_barrier(jnp.sum(weights, axis=2)).T
    query_feat = feature_map(queries)
    key_feat = feature_map(keys_in)
    carried = (seg_rows == last_seen).astype(jnp.float32)
    carried_num = jnp.einsum('thf,hfv->thv', low(query_feat), low(states), precision=HIGHEST) * carried[:, None, None]
    carried_den = jnp.einsum('thf,hf->th', query_feat, totals, precision=HIGHEST) * carried[:, None]
    numerator = low_back(local_num + carried_num)
    denominator = jnp.maximum(local_den + carried_den, 1.0)
    output = numerator / denominator[:, :, None]
    tail_id = seg_rows[row_count - 1]
    own_rows = (seg_rows == tail_id).astype(jnp.float32) * keep_rows
    new_states = jnp.einsum('thf,thv->hfv', low(key_feat) * own_rows[:, None, None], values, precision=HIGHEST) + carried[row_count - 1] * states
    new_totals = jnp.einsum('thf,t->hf', key_feat, own_rows, precision=HIGHEST) + carried[row_count - 1] * totals
    return ((new_states, new_totals, tail_id), output)

def layer(tokens, norm_gain, conv_taps, mix_in, mix_out, ffn_gain, ffn_in, ffn_out, seg_ids, keep_rows):
    scale_in = lax.rsqrt(lax.optimization_barrier(jnp.mean(tokens * tokens, axis=1, keepdims=True)) + EPSILON)
    normed = tokens * scale_in * norm_gain
    zero_row = jnp.zeros_like(normed[:1])
    back_one = jnp.concatenate([zero_row, normed[:-1]], axis=0)
    back_two = jnp.concatenate([zero_row, zero_row, normed[:-2]], axis=0)
    same_one = jnp.concatenate([jnp.zeros((1,), dtype=bool), seg_ids[1:] == seg_ids[:-1]])
    same_two = jnp.concatenate([jnp.zeros((2,), dtype=bool), seg_ids[2:] == seg_ids[:-2]])
    back_one = jnp.where(same_one[:, None], back_one, 0.0)
    back_two = jnp.where(same_two[:, None], back_two, 0.0)
    conv_out = conv_taps[:, 0] * normed + conv_taps[:, 1] * back_one + conv_taps[:, 2] * back_two
    mixed = low(conv_out * jax.nn.silu(normed))
    projected = low_back(jnp.dot(mixed, mix_in, precision=HIGHEST))
    qk_width = HEADS * FEAT
    queries = low(projected[:, :qk_width]).reshape(-1, TOK_DEV, HEADS, FEAT)
    keys_in = low(projected[:, qk_width:2 * qk_width]).reshape(-1, TOK_DEV, HEADS, FEAT)
    values = low(projected[:, 2 * qk_width:]).reshape(-1, TOK_DEV, HEADS, VDIM)
    start_carry = (jnp.zeros((HEADS, PHI, VDIM), jnp.float32), jnp.zeros((HEADS, PHI), jnp.float32), jnp.int32(-1))
    block_ids = seg_ids.reshape(-1, TOK_DEV)
    block_keep = keep_rows.reshape(-1, TOK_DEV)
    ignored, outputs = lax.scan(jax.checkpoint(attend_block), start_carry, (queries, keys_in, values, block_ids, block_keep))
    attended = low(outputs.reshape(-1, HEADS * VDIM))
    branch = low_back(jnp.dot(attended, mix_out, precision=HIGHEST))
    residual = tokens + branch
    scale_mid = lax.rsqrt(lax.optimization_barrier(jnp.mean(residual * residual, axis=1, keepdims=True)) + EPSILON)
    normed_mid = low(residual * scale_mid * ffn_gain)
    gate_val = low_back(jnp.dot(normed_mid, ffn_in[:, :D].T, precision=HIGHEST))
    up_val = low_back(jnp.dot(normed_mid, ffn_in[:, D:].T, precision=HIGHEST))
    activation = low(jax.nn.silu(gate_val) * up_val)
    ffn_result = low_back(jnp.dot(activation, ffn_out, precision=HIGHEST))
    return (residual + ffn_result, (branch, ffn_result))

def reference(tokens, seg_ids, valid_mask, norm_gain, conv_taps, mix_in, mix_out, ffn_gain, ffn_in, ffn_out, grad_out):
    keep_rows = valid_mask.astype(jnp.float32)
    x_full = tokens.astype(jnp.float32)

    def forward(x_in, gain_in, taps_in, proj_in, proj_out, gain_mid, hidden_in, hidden_out):
        return layer(x_in, gain_in, taps_in, proj_in, proj_out, gain_mid, hidden_in, hidden_out, seg_ids, keep_rows)
    result, pullback, extras = jax.vjp(forward, x_full, norm_gain, conv_taps, mix_in.astype(jnp.float32), mix_out.astype(jnp.float32), ffn_gain, ffn_in.astype(jnp.float32), ffn_out.astype(jnp.float32), has_aux=True)
    grads = pullback(grad_out.astype(jnp.float32))
    branch, ffn_result = extras
    valid_count = jnp.maximum(jnp.sum(keep_rows), 1.0)

    def root_mean(values):
        return jnp.sqrt(jnp.sum(keep_rows * lax.optimization_barrier(jnp.sum(values * values, axis=1))) / (valid_count * D))
    layer_stats = jnp.stack([root_mean(x_full), root_mean(branch), root_mean(ffn_result)])
    return (result.astype(jnp.bfloat16), grads[0].astype(jnp.bfloat16), grads[1], grads[2], grads[3], grads[4], grads[5], grads[6], grads[7], layer_stats)
```

```python
import functools
import math

import jax
import jax.numpy as jnp
import numpy as np
from jax import lax
from jax.experimental import pallas as pl
from jax.experimental.pallas import tpu as pltpu
from jax.sharding import PartitionSpec as P

HEADS = 16
FEAT = 16
VDIM = 112
PAIRS = FEAT * (FEAT + 1) // 2
FROWS = 160
LANES = 128
EXT = 32
EPSILON = 1e-05
OUTER_SCALE = 0.25 / math.sqrt(2.0)
BF = jnp.bfloat16
F32 = jnp.float32
VMEM_LIMIT = 50 * 1024 * 1024


def feature_tables():
    left = np.zeros((FROWS, EXT), np.float32)
    right = np.zeros((FROWS, EXT), np.float32)
    key_scale = np.zeros((FROWS, 1), np.float32)
    query_scale = np.zeros((FROWS, 1), np.float32)
    row = 0
    for i in range(FEAT):
        for j in range(i, FEAT):
            left[row, i] = 1.0
            right[row, j] = 1.0
            key_scale[row] = OUTER_SCALE
            query_scale[row] = OUTER_SCALE * (1.0 if i == j else 2.0)
            row += 1
    for i in range(FEAT):
        left[row, i] = 1.0
        right[row, FEAT] = 1.0
        key_scale[row] = query_scale[row] = 0.5
        row += 1
    left[row, FEAT] = right[row, FEAT] = 1.0
    key_scale[row] = query_scale[row] = 1.0
    return left, right, key_scale, query_scale


def dot(left, right, left_dim, right_dim):
    return lax.dot_general(
        left, right, (((left_dim,), (right_dim,)), ((), ())), preferred_element_type=F32
    )


def extended(vectors):
    rows = lax.broadcasted_iota(jnp.int32, (EXT - FEAT, vectors.shape[1]), 0)
    return jnp.concatenate([vectors, jnp.where(rows == 0, 1.0, 0.0).astype(BF)], axis=0)


def feature_parts(vectors, left, right):
    ext = extended(vectors)
    return dot(left, ext, 1, 0), dot(right, ext, 1, 0)


def padded_values(values):
    return jnp.concatenate(
        [values, jnp.zeros((LANES - VDIM, values.shape[1]), values.dtype)], axis=0
    )


def with_totals(state, total, high_id=None, low_id=None):
    lane = lax.broadcasted_iota(jnp.int32, state.shape, 1)
    high = total.astype(BF).astype(F32)
    out = jnp.where(lane == VDIM, high, state)
    out = jnp.where(lane == VDIM + 1, total - high, out)
    if high_id is not None:
        out = jnp.where(lane == VDIM + 2, high_id, out)
        out = jnp.where(lane == VDIM + 3, low_id, out)
    return out.astype(BF)


def total_of(state):
    lane = lax.broadcasted_iota(jnp.int32, state.shape, 1)
    return jnp.sum(
        jnp.where((lane == VDIM) | (lane == VDIM + 1), state, 0.0), axis=1, keepdims=True
    )


def state_kernel(ids_ref, keys_ref, values_ref, own_ref, left_ref, right_ref, scale_ref, out_ref):
    one, two = feature_parts(keys_ref[...], left_ref[...], right_ref[...])
    feats = one * two * scale_ref[...] * own_ref[...]
    state = dot(feats.astype(BF), padded_values(values_ref[...]), 1, 1)
    total = jnp.sum(feats, axis=1, keepdims=True)
    out_ref[0] = with_totals(state, total, ids_ref[0], ids_ref[1])


def tiles_of(count):
    half = count // 2
    return [(0, half, half), (half, count - half, count)]


def local_kernel(queries_ref, keys_ref, values_ref, allowed_ref, num_ref, den_ref):
    count = queries_ref.shape[1]
    for begin, width, seen in tiles_of(count):
        span = pl.ds(begin, width)
        scores = dot(keys_ref[:, :seen], queries_ref[:, span], 0, 0) * 0.25
        weights = (1.0 + scores + 0.5 * scores * scores) * allowed_ref[:seen, span]
        num_ref[:, span] = dot(values_ref[:, :seen], weights.astype(BF), 1, 0)
        den_ref[0, :, span] = jnp.sum(weights, axis=0, keepdims=True)


def carried_kernel(
    marks_ref, queries_ref, gathered_ref, num_ref, den_ref, cont_ref, left_ref, right_ref,
    scale_ref, attended_ref, output_ref, denom_ref, state_ref,
):
    blocks = gathered_ref.shape[0]
    state = gathered_ref[0, 0].astype(F32) * marks_ref[0]
    for block in range(1, blocks):
        state = state + gathered_ref[block, 0].astype(F32) * marks_ref[block]
    state_ref[0] = state
    total = total_of(state)
    one, two = feature_parts(queries_ref[...], left_ref[...], right_ref[...])
    feats = one * two * scale_ref[...]
    cont = cont_ref[...]
    extra = dot(state.astype(BF), feats.astype(BF), 0, 0)[:VDIM]
    denom = den_ref[0] + cont * jnp.sum(feats * total, axis=0, keepdims=True)
    output = (num_ref[...] + cont * extra) / jnp.maximum(denom, 1.0)
    output_ref[...] = output
    attended_ref[...] = output.astype(BF)
    denom_ref[0] = denom


def state_grad_kernel(
    grad_ref, output_ref, denom_ref, queries_ref, cont_ref, left_ref, right_ref, scale_ref,
    out_ref, dnum_ref, dden_ref,
):
    denom = denom_ref[0]
    floor = jnp.maximum(denom, 1.0)
    grad = grad_ref[...]
    dnum = (grad / floor).astype(BF)
    dden = jnp.where(
        denom > 1.0, -jnp.sum(grad * output_ref[...], axis=0, keepdims=True) / floor, 0.0
    )
    dnum_ref[...] = dnum
    dden_ref[0] = dden
    cont = cont_ref[...]
    one, two = feature_parts(queries_ref[...], left_ref[...], right_ref[...])
    feats = one * two * scale_ref[...]
    state = dot(feats.astype(BF), padded_values(dnum * cont.astype(BF)), 1, 1)
    total = jnp.sum(feats * (cont * dden), axis=1, keepdims=True)
    out_ref[0] = with_totals(state, total)


def feature_back(grads, one, two, scale, left_t, right_t):
    scaled = grads * scale
    return (
        dot(left_t, (scaled * two).astype(BF), 1, 0) + dot(right_t, (scaled * one).astype(BF), 1, 0)
    )[:FEAT]


def local_grad_kernel(
    queries_ref, keys_ref, values_ref, dnum_ref, dden_ref, allowed_ref, state_ref, cont_ref,
    left_ref, right_ref, left_t_ref, right_t_ref, scale_ref, dq_ref, dk_ref, dv_ref,
):
    count = queries_ref.shape[1]
    state = state_ref[0]
    total = total_of(state)
    dnum = dnum_ref[...]
    one, two = feature_parts(queries_ref[...], left_ref[...], right_ref[...])
    grads = cont_ref[...] * (
        dot(state.astype(BF), padded_values(dnum), 1, 0) + total * dden_ref[0]
    )
    carried = feature_back(grads, one, two, scale_ref[...], left_t_ref[...], right_t_ref[...])
    for begin, width, seen in tiles_of(count):
        span = pl.ds(begin, width)
        keys = keys_ref[:, :seen]
        queries = queries_ref[:, span]
        scores = dot(keys, queries, 0, 0) * 0.25
        allowed = allowed_ref[:seen, span]
        weights = ((1.0 + scores + 0.5 * scores * scores) * allowed).astype(BF)
        dnum_part = dnum_ref[:, span]
        dweights = dot(values_ref[:, :seen], dnum_part, 0, 0) + dden_ref[0, :, span]
        dscores = (dweights * allowed * (1.0 + scores)).astype(BF)
        dq = dot(keys, dscores, 1, 0) * 0.25 + carried[:, begin : begin + width]
        dq_ref[:, span] = dq.astype(BF)
        dk = dot(queries, dscores, 1, 1) * 0.25
        dv = dot(dnum_part, weights, 1, 1)
        if begin == 0:
            dk_ref[:, :seen] = dk
            dv_ref[:, :seen] = dv
        else:
            dk_ref[:, :begin] += dk[:, :begin]
            dv_ref[:, :begin] += dv[:, :begin]
            dk_ref[:, span] = dk[:, begin:]
            dv_ref[:, span] = dv[:, begin:]


def late_grad_kernel(
    marks_ref, gathered_ref, keys_ref, values_ref, own_ref, dk_in_ref, dv_in_ref, left_ref,
    right_ref, left_t_ref, right_t_ref, scale_ref, dk_ref, dv_ref,
):
    blocks = gathered_ref.shape[0]
    state = gathered_ref[0, 0].astype(F32) * marks_ref[0]
    for block in range(1, blocks):
        state = state + gathered_ref[block, 0].astype(F32) * marks_ref[block]
    total = total_of(state)
    low = state.astype(BF)
    own = own_ref[...]
    one, two = feature_parts(keys_ref[...], left_ref[...], right_ref[...])
    feats = (one * two * scale_ref[...]).astype(BF)
    grads = own * (dot(low, padded_values(values_ref[...]), 1, 0) + total)
    back = feature_back(grads, one, two, scale_ref[...], left_t_ref[...], right_t_ref[...])
    dk_ref[...] = (dk_in_ref[...] + back).astype(BF)
    dv_ref[...] = (dv_in_ref[...] + own * dot(low, feats, 0, 0)[:VDIM]).astype(BF)


def ffn_kernel(x_ref, dy_ref, w_in_ref, w_out_ref, act_ref, gate_ref, up_ref, back_ref):
    width = x_ref.shape[1]
    x = x_ref[...]
    gate = dot(x, w_in_ref[:, :width], 1, 1)
    up = dot(x, w_in_ref[:, width:], 1, 1)
    dact = dot(dy_ref[...], w_out_ref[...], 1, 1)
    sigma = 1.0 / (1.0 + jnp.exp(-gate))
    silu = gate * sigma
    act_ref[...] = (silu * up).astype(BF)
    dgate = (dact * up * (sigma * (1.0 + gate * (1.0 - sigma)))).astype(BF)
    dup = (dact * silu).astype(BF)
    gate_ref[...] = dgate
    up_ref[...] = dup
    back_ref[...] = (
        dot(dgate, w_in_ref[:, :width], 1, 0) + dot(dup, w_in_ref[:, width:], 1, 0)
    ).astype(BF)


def ffn_grad_kernel(
    x_ref, dy_ref, act_ref, gate_ref, up_ref, w_out_ref, result_ref, grads_ref, total_ref
):
    width = x_ref.shape[1]
    step = pl.program_id(0)
    act = act_ref[...]
    result_ref[...] = dot(act, w_out_ref[...], 1, 0).astype(BF)
    terms = (
        (gate_ref[...], x_ref[...]),
        (up_ref[...], x_ref[...]),
        (act, dy_ref[...]),
    )
    for place, (left, right) in enumerate(terms):
        span = pl.ds(place * width, width)
        term = dot(left, right, 0, 0)

        @pl.when(step == 0)
        def _():
            total_ref[:, span] = term

        @pl.when(step > 0)
        def _():
            total_ref[:, span] += term

    @pl.when(step == pl.num_programs(0) - 1)
    def _():
        grads_ref[...] = total_ref[...].astype(BF)


def call(kernel, outs, grid, in_specs, out_specs, flops, moved, *args, scratch=()):
    return pl.pallas_call(
        kernel,
        out_shape=outs,
        grid=grid,
        in_specs=in_specs,
        out_specs=out_specs,
        scratch_shapes=list(scratch),
        compiler_params=pltpu.CompilerParams(vmem_limit_bytes=VMEM_LIMIT),
        cost_estimate=pl.CostEstimate(flops=flops, bytes_accessed=moved, transcendentals=0),
    )(*args)


def passed_along(block, axis, distance):
    devices = range(lax.axis_size(axis))
    route = [(i - distance, i) for i in devices if i - distance in devices]
    return lax.ppermute(block, axis, route)


def silu_grad(values):
    sigma = jax.nn.sigmoid(values)
    return sigma * (1.0 + values * (1.0 - sigma))


def row_scale(values):
    return lax.rsqrt(jnp.mean(values * values, axis=-1, keepdims=True) + EPSILON)


def rep_sum(terms):
    count = lax.axis_size("rep")
    mine = lax.axis_index("rep")
    rows = terms.shape[0] // count

    def part(index):
        return lax.dynamic_slice_in_dim(terms, lax.rem(index + count, count) * rows, rows, 0)

    total = part(mine).astype(F32)
    for shift in range(1, count):
        route = [(i, (i + shift) % count) for i in range(count)]
        total = total + lax.ppermute(part(mine + shift), "rep", route).astype(F32)
    low = total.astype(BF)
    whole = jnp.zeros(terms.shape, F32)
    whole = lax.dynamic_update_slice_in_dim(whole, low.astype(F32), mine * rows, 0)
    for shift in range(1, count):
        route = [(i, (i + shift) % count) for i in range(count)]
        other = lax.ppermute(low, "rep", route).astype(F32)
        whole = lax.dynamic_update_slice_in_dim(
            whole, other, lax.rem(mine - shift + count, count) * rows, 0
        )
    return whole


def body(
    tokens, seg_ids, valid_mask, norm_gain, conv_taps, mix_in, mix_out, ffn_gain, ffn_in, ffn_out,
    grad_out,
):
    row_count, model_width = tokens.shape
    group = lax.axis_size("grp")
    mine = lax.axis_index("grp")
    qk_width = HEADS * FEAT
    v_width = HEADS * VDIM
    hidden = ffn_in.shape[0]

    full_in = lax.all_gather(mix_in, "grp", axis=0, tiled=True)
    full_out = lax.all_gather(mix_out, "grp", axis=0, tiled=True)
    all_dy = lax.all_gather(grad_out, "grp", axis=0, tiled=True)

    x_full = tokens.astype(F32)
    id_float = seg_ids.astype(F32)
    keep_rows = valid_mask.astype(F32)
    edge = jnp.concatenate([x_full[row_count - 2 :], id_float[row_count - 2 :, None]], axis=1)
    edge = passed_along(edge, "grp", 1)
    ext_x = jnp.concatenate([edge[:, :model_width], x_full], axis=0)
    ext_ids = jnp.concatenate([edge[:, model_width], id_float], axis=0)
    ext_scale = row_scale(ext_x)
    ext_unit = ext_x * ext_scale
    ext_norm = ext_unit * norm_gain
    normed = ext_norm[2:]
    unit_in = ext_unit[2:]
    scale_in = ext_scale[2:]
    same_one = (ext_ids[1 : row_count + 1] == id_float).astype(F32)[:, None]
    same_two = (ext_ids[:row_count] == id_float).astype(F32)[:, None]
    back_one = ext_norm[1 : row_count + 1] * same_one
    back_two = ext_norm[:row_count] * same_two
    conv_out = conv_taps[:, 0] * normed + conv_taps[:, 1] * back_one + conv_taps[:, 2] * back_two
    gated = jax.nn.silu(normed)
    mixed = (conv_out * gated).astype(BF)

    positions = jnp.arange(row_count)
    allowed = (
        (positions[:, None] <= positions[None, :]) & (seg_ids[:, None] == seg_ids[None, :])
    ).astype(F32) * keep_rows[:, None]
    last_id = seg_ids[row_count - 1]
    own = ((seg_ids == last_id).astype(F32) * keep_rows)[None, :]
    left, right, key_scale, query_scale = feature_tables()
    left_low, right_low = jnp.asarray(left, BF), jnp.asarray(right, BF)
    left_t, right_t = jnp.asarray(left.T, BF), jnp.asarray(right.T, BF)
    key_scale, query_scale = jnp.asarray(key_scale), jnp.asarray(query_scale)

    def whole(*shape):
        return pl.BlockSpec(shape, lambda h: (0,) * len(shape))

    smem = pl.BlockSpec(memory_space=pltpu.SMEM)
    qk_spec = pl.BlockSpec((FEAT, row_count), lambda h: (h, 0))
    k_spec = pl.BlockSpec((FEAT, row_count), lambda h: (HEADS + h, 0))
    v_spec = pl.BlockSpec((VDIM, row_count), lambda h: (h, 0))
    row_spec = pl.BlockSpec((1, 1, row_count), lambda h: (h, 0, 0))
    state_spec = pl.BlockSpec((1, FROWS, LANES), lambda h: (h, 0, 0))
    all_states_spec = pl.BlockSpec((group, 1, FROWS, LANES), lambda h: (0, h, 0, 0))
    one_row = whole(1, row_count)
    square = whole(row_count, row_count)
    table = whole(FROWS, EXT)
    table_t = whole(EXT, FROWS)
    column = whole(FROWS, 1)
    grid = (HEADS,)
    v_low = jax.ShapeDtypeStruct((v_width, row_count), BF)
    v_wide = jax.ShapeDtypeStruct((v_width, row_count), F32)
    qk_low = jax.ShapeDtypeStruct((qk_width, row_count), BF)
    qk_wide = jax.ShapeDtypeStruct((qk_width, row_count), F32)
    head_rows = jax.ShapeDtypeStruct((HEADS, 1, row_count), F32)
    states_low = jax.ShapeDtypeStruct((HEADS, FROWS, LANES), BF)
    states_wide = jax.ShapeDtypeStruct((HEADS, FROWS, LANES), F32)

    qk = dot(full_in[:, : 2 * qk_width], mixed, 0, 1).astype(BF)
    values = dot(full_in[:, 2 * qk_width :], mixed, 0, 1).astype(BF)

    id_pieces = jnp.stack([last_id // 256, last_id % 256]).astype(F32)
    states = call(
        state_kernel, states_low, grid,
        [smem, k_spec, v_spec, one_row, table, table, column], state_spec,
        10**9, 4 * 10**6,
        id_pieces, qk, values, own, left_low, right_low, key_scale,
    )
    all_states = lax.all_gather(states, "grp", axis=0)
    num_local, den_local = call(
        local_kernel, (v_wide, head_rows), grid,
        [qk_spec, k_spec, v_spec, square], (v_spec, row_spec),
        15 * 10**9, 7 * 10**6,
        qk, qk, values, allowed,
    )
    id_parts = all_states[:, 0, 0, VDIM + 2 : VDIM + 4].astype(F32)
    last_ids = id_parts[:, 0] * 256.0 + id_parts[:, 1]
    order = jnp.arange(group)
    before = jnp.where(mine > 0, last_ids[jnp.maximum(mine - 1, 0)], -1.0)
    marks = ((order < mine) & (last_ids == before)).astype(F32)
    cont = (id_float == before).astype(F32)[None, :]
    attended, output, denom, state_in = call(
        carried_kernel, (v_low, v_wide, head_rows, states_wide), grid,
        [smem, qk_spec, all_states_spec, v_spec, row_spec, one_row, table, table, column],
        (v_spec, v_spec, row_spec, state_spec),
        2 * 10**9, 16 * 10**6,
        marks, qk, all_states, num_local, den_local, cont, left_low, right_low, query_scale,
    )
    branch = dot(attended, full_out, 0, 0)
    residual = x_full + branch
    scale_mid = row_scale(residual)
    unit_mid = residual * scale_mid
    normed_mid = (unit_mid * ffn_gain).astype(BF)

    all_mid = lax.all_gather(normed_mid, "grp", axis=0, tiled=True)
    tile = row_count
    steps = group
    wide_tile = pl.BlockSpec((tile, model_width), lambda i: (i, 0))
    thin_tile = pl.BlockSpec((tile, hidden), lambda i: (i, 0))
    thin = jax.ShapeDtypeStruct((row_count * group, hidden), BF)
    wide = jax.ShapeDtypeStruct((row_count * group, model_width), BF)
    w_in_spec = whole(hidden, 2 * model_width)
    w_out_spec = whole(hidden, model_width)
    unit = 2 * row_count * group * hidden * model_width
    activation, dgate, dup, back_terms = call(
        ffn_kernel, (thin, thin, thin, wide), (steps,),
        [wide_tile, wide_tile, w_in_spec, w_out_spec],
        (thin_tile, thin_tile, thin_tile, wide_tile),
        5 * unit, 60 * 10**6,
        all_mid, all_dy, ffn_in, ffn_out,
    )
    grad_normed_mid = lax.psum_scatter(
        back_terms, "grp", scatter_dimension=0, tiled=True
    ).astype(F32)
    result_terms, ffn_grads = call(
        ffn_grad_kernel, (wide, jax.ShapeDtypeStruct((hidden, 3 * model_width), BF)), (steps,),
        [wide_tile, wide_tile, thin_tile, thin_tile, thin_tile, w_out_spec],
        (wide_tile, whole(hidden, 3 * model_width)),
        4 * unit, 60 * 10**6,
        all_mid, all_dy, activation, dgate, dup, ffn_out,
        scratch=[pltpu.VMEM((hidden, 3 * model_width), F32)],
    )
    ffn_result = lax.psum_scatter(
        result_terms, "grp", scatter_dimension=0, tiled=True
    ).astype(F32)
    mixed_out = (residual + ffn_result).astype(BF)
    ffn_grads = rep_sum(ffn_grads)

    grad_y = grad_out.astype(F32)
    grad_unit_mid = grad_normed_mid * ffn_gain
    grad_ffn_gain = jnp.sum(grad_normed_mid * unit_mid, axis=0)
    grad_mid = grad_y + scale_mid * (
        grad_unit_mid - unit_mid * jnp.mean(grad_unit_mid * unit_mid, axis=1, keepdims=True)
    )
    grad_branch = grad_mid.astype(BF)
    grad_att = dot(full_out, grad_branch, 1, 1)
    out_terms = dot(attended, grad_branch, 1, 0).astype(BF)
    out_shard = lax.psum_scatter(out_terms, "grp", scatter_dimension=0, tiled=True)
    grad_mix_out = rep_sum(out_shard)

    state_grads, dnum, dden = call(
        state_grad_kernel, (states_low, v_low, head_rows), grid,
        [v_spec, v_spec, row_spec, qk_spec, one_row, table, table, column],
        (state_spec, v_spec, row_spec),
        2 * 10**9, 12 * 10**6,
        grad_att, output, denom, qk, cont, left_low, right_low, query_scale,
    )
    all_state_grads = lax.all_gather(state_grads, "grp", axis=0)
    grad_queries, dk_local, dv_local = call(
        local_grad_kernel, (qk_low, qk_wide, v_wide), grid,
        [qk_spec, k_spec, v_spec, v_spec, row_spec, square, state_spec, one_row,
         table, table, table_t, table_t, column],
        (qk_spec, qk_spec, v_spec),
        30 * 10**9, 12 * 10**6,
        qk, qk, values, dnum, dden, allowed, state_in, cont,
        left_low, right_low, left_t, right_t, query_scale,
    )
    previous_ids = jnp.concatenate([jnp.full((1,), -1.0, F32), last_ids[:-1]])
    late_marks = ((order > mine) & (previous_ids == last_ids[mine])).astype(F32)
    grad_keys, grad_values = call(
        late_grad_kernel, (qk_low, v_low), grid,
        [smem, all_states_spec, k_spec, v_spec, one_row, qk_spec, v_spec,
         table, table, table_t, table_t, column],
        (qk_spec, v_spec),
        2 * 10**9, 14 * 10**6,
        late_marks, all_state_grads, qk, values, own, dk_local, dv_local,
        left_low, right_low, left_t, right_t, key_scale,
    )
    grad_projected = jnp.concatenate([grad_queries, grad_keys, grad_values], axis=0)
    in_terms = dot(mixed, grad_projected, 0, 1).astype(BF)
    in_shard = lax.psum_scatter(in_terms, "grp", scatter_dimension=0, tiled=True)
    grad_mix_in = rep_sum(in_shard)

    grad_mixed = dot(grad_projected, full_in, 0, 1)
    grad_conv = grad_mixed * gated
    grad_normed = grad_mixed * conv_out * silu_grad(normed)
    edge_back = jnp.concatenate([grad_conv[:2], id_float[:2, None]], axis=1)
    edge_back = passed_along(edge_back, "grp", -1)
    ext_grad = jnp.concatenate([grad_conv, edge_back[:, :model_width]], axis=0)
    ext_grad_ids = jnp.concatenate([id_float, edge_back[:, model_width]], axis=0)
    ahead_one = (ext_grad_ids[1 : row_count + 1] == id_float).astype(F32)[:, None]
    ahead_two = (ext_grad_ids[2:] == id_float).astype(F32)[:, None]
    grad_normed = (
        grad_normed
        + conv_taps[:, 0] * grad_conv
        + conv_taps[:, 1] * (ext_grad[1 : row_count + 1] * ahead_one)
        + conv_taps[:, 2] * (ext_grad[2:] * ahead_two)
    )
    grad_unit_in = grad_normed * norm_gain
    grad_tokens = (
        grad_mid
        + scale_in
        * (grad_unit_in - unit_in * jnp.mean(grad_unit_in * unit_in, axis=1, keepdims=True))
    ).astype(BF)

    stat_terms = jnp.stack(
        [
            jnp.sum(keep_rows * jnp.sum(x_full * x_full, axis=1)),
            jnp.sum(keep_rows * jnp.sum(branch * branch, axis=1)),
            jnp.sum(keep_rows * jnp.sum(ffn_result * ffn_result, axis=1)),
            jnp.sum(keep_rows),
        ]
    )
    small = jnp.concatenate(
        [
            jnp.sum(grad_normed * unit_in, axis=0),
            jnp.sum(grad_conv * normed, axis=0),
            jnp.sum(grad_conv * back_one, axis=0),
            jnp.sum(grad_conv * back_two, axis=0),
            grad_ffn_gain,
            stat_terms,
        ]
    )
    small = jnp.pad(small, (0, -small.shape[0] % 1024)).reshape(-1, LANES)
    small = jnp.sum(lax.all_gather(small, ("rep", "grp"), axis=0), axis=0).reshape(-1)
    rows = small[: 5 * model_width].reshape(5, model_width)
    stats = small[5 * model_width : 5 * model_width + 4]
    layer_stats = jnp.sqrt(stats[:3] / (jnp.maximum(stats[3], 1.0) * model_width))
    return (
        mixed_out,
        grad_tokens,
        rows[0],
        rows[1:4].T,
        grad_mix_in,
        grad_mix_out,
        rows[4],
        ffn_grads[:, : 2 * model_width],
        ffn_grads[:, 2 * model_width :],
        layer_stats,
    )


def solution(mesh):
    split = P(("rep", "grp"), None)
    shard = P("grp", None)
    return jax.shard_map(
        body,
        mesh=mesh,
        in_specs=(
            split, P(("rep", "grp")), P(("rep", "grp")), P(), P(), shard, shard, P(), shard, shard,
            split,
        ),
        out_specs=(split, split, P(), P(), shard, shard, P(), shard, shard, P()),
        check_vma=False,
    )
```

```python
import functools
import math

import jax
import jax.numpy as jnp
import numpy as np
from jax import lax
from jax.experimental import pallas as pl
from jax.experimental.pallas import tpu as pltpu
from jax.sharding import PartitionSpec as P

HEADS = 16
FEAT = 16
VDIM = 112
PAIRS = FEAT * (FEAT + 1) // 2
FROWS = 160
LANES = 128
EXT = 32
EPSILON = 1e-05
OUTER_SCALE = 0.25 / math.sqrt(2.0)
BF = jnp.bfloat16
F32 = jnp.float32
VMEM_LIMIT = 50 * 1024 * 1024


def feature_tables():
    left = np.zeros((FROWS, EXT), np.float32)
    right = np.zeros((FROWS, EXT), np.float32)
    key_scale = np.zeros((FROWS, 1), np.float32)
    query_scale = np.zeros((FROWS, 1), np.float32)
    row = 0
    for i in range(FEAT):
        for j in range(i, FEAT):
            left[row, i] = 1.0
            right[row, j] = 1.0
            key_scale[row] = OUTER_SCALE
            query_scale[row] = OUTER_SCALE * (1.0 if i == j else 2.0)
            row += 1
    for i in range(FEAT):
        left[row, i] = 1.0
        right[row, FEAT] = 1.0
        key_scale[row] = query_scale[row] = 0.5
        row += 1
    left[row, FEAT] = right[row, FEAT] = 1.0
    key_scale[row] = query_scale[row] = 1.0
    return left, right, key_scale, query_scale


def dot(left, right, left_dim, right_dim):
    return lax.dot_general(
        left, right, (((left_dim,), (right_dim,)), ((), ())), preferred_element_type=F32
    )


def extended(vectors):
    rows = lax.broadcasted_iota(jnp.int32, (EXT - FEAT, vectors.shape[1]), 0)
    return jnp.concatenate([vectors, jnp.where(rows == 0, 1.0, 0.0).astype(BF)], axis=0)


def feature_parts(vectors, left, right):
    ext = extended(vectors)
    return dot(left, ext, 1, 0), dot(right, ext, 1, 0)


def padded_values(values):
    return jnp.concatenate(
        [values, jnp.zeros((LANES - VDIM, values.shape[1]), values.dtype)], axis=0
    )


def with_totals(state, total, high_id=None, low_id=None):
    lane = lax.broadcasted_iota(jnp.int32, state.shape, 1)
    high = total.astype(BF).astype(F32)
    out = jnp.where(lane == VDIM, high, state)
    out = jnp.where(lane == VDIM + 1, total - high, out)
    if high_id is not None:
        out = jnp.where(lane == VDIM + 2, high_id, out)
        out = jnp.where(lane == VDIM + 3, low_id, out)
    return out.astype(BF)


def total_of(state):
    lane = lax.broadcasted_iota(jnp.int32, state.shape, 1)
    return jnp.sum(
        jnp.where((lane == VDIM) | (lane == VDIM + 1), state, 0.0), axis=1, keepdims=True
    )


def state_kernel(ids_ref, keys_ref, values_ref, own_ref, left_ref, right_ref, scale_ref, out_ref):
    one, two = feature_parts(keys_ref[...], left_ref[...], right_ref[...])
    feats = one * two * scale_ref[...] * own_ref[...]
    state = dot(feats.astype(BF), padded_values(values_ref[...]), 1, 1)
    total = jnp.sum(feats, axis=1, keepdims=True)
    out_ref[0] = with_totals(state, total, ids_ref[0], ids_ref[1])


def tiles_of(count):
    half = count // 2
    return [(0, half, half), (half, count - half, count)]


def local_kernel(queries_ref, keys_ref, values_ref, allowed_ref, num_ref, den_ref):
    count = queries_ref.shape[1]
    for begin, width, seen in tiles_of(count):
        span = pl.ds(begin, width)
        scores = dot(keys_ref[:, :seen], queries_ref[:, span], 0, 0) * 0.25
        weights = (1.0 + scores + 0.5 * scores * scores) * allowed_ref[:seen, span]
        num_ref[:, span] = dot(values_ref[:, :seen], weights.astype(BF), 1, 0)
        den_ref[0, :, span] = jnp.sum(weights, axis=0, keepdims=True)


def marked_sum(marks_ref, gathered_refs):
    place = 0
    total = None
    for ref in gathered_refs:
        for slot in range(ref.shape[0]):
            term = ref[slot, 0].astype(F32) * marks_ref[place]
            total = term if total is None else total + term
            place += 1
    return total


def carried_kernel(stacks, marks_ref, *refs):
    gathered_refs = refs[:stacks]
    (queries_ref, num_ref, den_ref, cont_ref, left_ref, right_ref,
     scale_ref, attended_ref, output_ref, denom_ref, state_ref) = refs[stacks:]
    state = marked_sum(marks_ref, gathered_refs)
    state_ref[0] = state
    total = total_of(state)
    one, two = feature_parts(queries_ref[...], left_ref[...], right_ref[...])
    feats = one * two * scale_ref[...]
    cont = cont_ref[...]
    extra = dot(state.astype(BF), feats.astype(BF), 0, 0)[:VDIM]
    denom = den_ref[0] + cont * jnp.sum(feats * total, axis=0, keepdims=True)
    output = (num_ref[...] + cont * extra) / jnp.maximum(denom, 1.0)
    output_ref[...] = output
    attended_ref[...] = output.astype(BF)
    denom_ref[0] = denom


def state_grad_kernel(
    grad_ref, output_ref, denom_ref, queries_ref, cont_ref, left_ref, right_ref, scale_ref,
    out_ref, dnum_ref, dden_ref,
):
    denom = denom_ref[0]
    floor = jnp.maximum(denom, 1.0)
    grad = grad_ref[...]
    dnum = (grad / floor).astype(BF)
    dden = jnp.where(
        denom > 1.0, -jnp.sum(grad * output_ref[...], axis=0, keepdims=True) / floor, 0.0
    )
    dnum_ref[...] = dnum
    dden_ref[0] = dden
    cont = cont_ref[...]
    one, two = feature_parts(queries_ref[...], left_ref[...], right_ref[...])
    feats = one * two * scale_ref[...]
    state = dot(feats.astype(BF), padded_values(dnum * cont.astype(BF)), 1, 1)
    total = jnp.sum(feats * (cont * dden), axis=1, keepdims=True)
    out_ref[0] = with_totals(state, total)


def feature_back(grads, one, two, scale, left_t, right_t):
    scaled = grads * scale
    return (
        dot(left_t, (scaled * two).astype(BF), 1, 0) + dot(right_t, (scaled * one).astype(BF), 1, 0)
    )[:FEAT]


def local_grad_kernel(
    queries_ref, keys_ref, values_ref, dnum_ref, dden_ref, allowed_ref, state_ref, cont_ref,
    left_ref, right_ref, left_t_ref, right_t_ref, scale_ref, dq_ref, dk_ref, dv_ref,
):
    count = queries_ref.shape[1]
    state = state_ref[0]
    total = total_of(state)
    dnum = dnum_ref[...]
    one, two = feature_parts(queries_ref[...], left_ref[...], right_ref[...])
    grads = cont_ref[...] * (
        dot(state.astype(BF), padded_values(dnum), 1, 0) + total * dden_ref[0]
    )
    carried = feature_back(grads, one, two, scale_ref[...], left_t_ref[...], right_t_ref[...])
    for begin, width, seen in tiles_of(count):
        span = pl.ds(begin, width)
        keys = keys_ref[:, :seen]
        queries = queries_ref[:, span]
        scores = dot(keys, queries, 0, 0) * 0.25
        allowed = allowed_ref[:seen, span]
        weights = ((1.0 + scores + 0.5 * scores * scores) * allowed).astype(BF)
        dnum_part = dnum_ref[:, span]
        dweights = dot(values_ref[:, :seen], dnum_part, 0, 0) + dden_ref[0, :, span]
        dscores = (dweights * allowed * (1.0 + scores)).astype(BF)
        dq = dot(keys, dscores, 1, 0) * 0.25 + carried[:, begin : begin + width]
        dq_ref[:, span] = dq.astype(BF)
        dk = dot(queries, dscores, 1, 1) * 0.25
        dv = dot(dnum_part, weights, 1, 1)
        if begin == 0:
            dk_ref[:, :seen] = dk
            dv_ref[:, :seen] = dv
        else:
            dk_ref[:, :begin] += dk[:, :begin]
            dv_ref[:, :begin] += dv[:, :begin]
            dk_ref[:, span] = dk[:, begin:]
            dv_ref[:, span] = dv[:, begin:]


def late_grad_kernel(stacks, marks_ref, *refs):
    gathered_refs = refs[:stacks]
    (keys_ref, values_ref, own_ref, dk_in_ref, dv_in_ref, left_ref, right_ref, left_t_ref,
     right_t_ref, scale_ref, dk_ref, dv_ref) = refs[stacks:]
    state = marked_sum(marks_ref, gathered_refs)
    total = total_of(state)
    low = state.astype(BF)
    own = own_ref[...]
    one, two = feature_parts(keys_ref[...], left_ref[...], right_ref[...])
    feats = (one * two * scale_ref[...]).astype(BF)
    grads = own * (dot(low, padded_values(values_ref[...]), 1, 0) + total)
    back = feature_back(grads, one, two, scale_ref[...], left_t_ref[...], right_t_ref[...])
    dk_ref[...] = (dk_in_ref[...] + back).astype(BF)
    dv_ref[...] = (dv_in_ref[...] + own * dot(low, feats, 0, 0)[:VDIM]).astype(BF)


def ffn_kernel(x_ref, dy_ref, w_in_ref, w_out_ref, act_ref, pre_ref, back_ref):
    width = x_ref.shape[1]
    x = x_ref[...]
    gate = dot(x, w_in_ref[:, :width], 1, 1)
    up = dot(x, w_in_ref[:, width:], 1, 1)
    dact = dot(dy_ref[...], w_out_ref[...], 1, 1)
    sigma = 1.0 / (1.0 + jnp.exp(-gate))
    silu = gate * sigma
    act_ref[0] = (silu * up).astype(BF)
    dgate = (dact * up * (sigma * (1.0 + gate * (1.0 - sigma)))).astype(BF)
    dup = (dact * silu).astype(BF)
    pre_ref[0] = dgate
    pre_ref[1] = dup
    back_ref[...] = (
        dot(dgate, w_in_ref[:, :width], 1, 0) + dot(dup, w_in_ref[:, width:], 1, 0)
    ).astype(BF)


def weight_grad_kernel(pieces, *refs):
    lefts, rights, outs = refs[:pieces], refs[pieces : 2 * pieces], refs[2 * pieces :]
    total = None
    for left, right in zip(lefts, rights):
        term = dot(left[0], right[...], 0, 0)
        total = term if total is None else total + term
    rows = outs[0].shape[0]
    for place, out_ref in enumerate(outs):
        out_ref[...] = total[place * rows : (place + 1) * rows].astype(BF)


def mid_grad_kernel(terms, *refs):
    term_refs = refs[:terms]
    residual_ref, grad_ref, gain_ref, mid_ref, branch_ref, gain_grad_ref = refs[terms:]
    grad = term_refs[0][...].astype(F32)
    for term_ref in term_refs[1:]:
        grad = grad + term_ref[...].astype(F32)
    residual = residual_ref[...]
    scale = lax.rsqrt(jnp.mean(residual * residual, axis=1, keepdims=True) + EPSILON)
    unit = residual * scale
    product = grad * unit
    part = jnp.sum(product, axis=0, keepdims=True)
    step = pl.program_id(0)

    @pl.when(step == 0)
    def _():
        gain_grad_ref[...] = part

    @pl.when(step > 0)
    def _():
        gain_grad_ref[...] += part

    gain = gain_ref[...]
    mean = jnp.mean(product * gain, axis=1, keepdims=True)
    mid = grad_ref[...].astype(F32) + scale * (grad * gain - unit * mean)
    mid_ref[...] = mid
    branch_ref[...] = mid.astype(BF)


def conv_grad_kernel(
    x_ref, before_ref, after_ref, scale_ref, flags_ref, gain_ref, taps_ref, mixed_ref, mid_ref,
    out_ref, sums_ref, scaled_ref,
):
    count, width = x_ref.shape
    cut = LANES
    row = lax.broadcasted_iota(jnp.int32, (count, cut), 0)

    def spread(column):
        return jnp.broadcast_to(column, (count, cut))

    scale = spread(scale_ref[...])
    same_one, same_two = spread(flags_ref[:, 0:1]), spread(flags_ref[:, 1:2])
    ahead_one, ahead_two = spread(flags_ref[:, 2:3]), spread(flags_ref[:, 3:4])

    def one_cut(index, total):
        span = pl.ds(pl.multiple_of(index * cut, cut), cut)
        gain = gain_ref[:, span]
        unit = x_ref[:, span].astype(F32) * scale
        normed = unit * gain
        older, newer = before_ref[0:1, span], before_ref[1:2, span]
        back_one = jnp.where(row == 0, newer, pltpu.roll(normed, 1, 0)) * same_one
        back_two = pltpu.roll(normed, 2, 0)
        back_two = jnp.where(row == 0, older, jnp.where(row == 1, newer, back_two)) * same_two
        tap_0, tap_1, tap_2 = taps_ref[0:1, span], taps_ref[1:2, span], taps_ref[2:3, span]
        conv = tap_0 * normed + tap_1 * back_one + tap_2 * back_two
        sigma = 1.0 / (1.0 + jnp.exp(-normed))
        mixed = mixed_ref[:, span]
        grad_conv = mixed * (normed * sigma)
        next_0, next_1 = after_ref[0:1, span], after_ref[1:2, span]
        on_one = jnp.where(row == count - 1, next_0, pltpu.roll(grad_conv, count - 1, 0))
        on_two = pltpu.roll(grad_conv, count - 2, 0)
        on_two = jnp.where(
            row == count - 2, next_0, jnp.where(row == count - 1, next_1, on_two)
        )
        grad = (
            mixed * conv * (sigma * (1.0 + normed * (1.0 - sigma)))
            + tap_0 * grad_conv
            + tap_1 * (on_one * ahead_one)
            + tap_2 * (on_two * ahead_two)
        )
        product = grad * unit
        sums_ref[0:1, span] = jnp.sum(product, axis=0, keepdims=True)
        sums_ref[1:2, span] = jnp.sum(grad_conv * normed, axis=0, keepdims=True)
        sums_ref[2:3, span] = jnp.sum(grad_conv * back_one, axis=0, keepdims=True)
        sums_ref[3:4, span] = jnp.sum(grad_conv * back_two, axis=0, keepdims=True)
        scaled_ref[:, span] = grad * gain
        return total + product * gain

    total = lax.fori_loop(0, width // cut, one_cut, jnp.zeros((count, cut), F32))
    mean = spread(jnp.sum(total, axis=1, keepdims=True) * (1.0 / width))

    def second(index, carry):
        span = pl.ds(pl.multiple_of(index * cut, cut), cut)
        unit = x_ref[:, span].astype(F32) * scale
        out_ref[:, span] = (mid_ref[:, span] + scale * (scaled_ref[:, span] - unit * mean)).astype(BF)
        return carry

    lax.fori_loop(0, width // cut, second, 0)


def call(kernel, outs, grid, in_specs, out_specs, flops, moved, *args, scratch=()):
    return pl.pallas_call(
        kernel,
        out_shape=outs,
        grid=grid,
        in_specs=in_specs,
        out_specs=out_specs,
        scratch_shapes=list(scratch),
        compiler_params=pltpu.CompilerParams(vmem_limit_bytes=VMEM_LIMIT),
        cost_estimate=pl.CostEstimate(flops=0, bytes_accessed=0, transcendentals=0),
    )(*args)


def passed_along(block, axis, distance):
    devices = range(lax.axis_size(axis))
    route = [(i - distance, i) for i in devices if i - distance in devices]
    return lax.ppermute(block, axis, route)


def silu_grad(values):
    sigma = jax.nn.sigmoid(values)
    return sigma * (1.0 + values * (1.0 - sigma))


def row_scale(values):
    return lax.rsqrt(jnp.mean(values * values, axis=-1, keepdims=True) + EPSILON)


def exchanged(block, offset):
    count = lax.axis_size("grp")
    return lax.ppermute(block, "grp", [(i, i ^ offset) for i in range(count)])


def paired():
    return lax.axis_size("grp") == 8


def gather_near(block):
    if not paired():
        offsets = list(range(lax.axis_size("grp")))
        return offsets, [block] + [exchanged(block, k) for k in offsets[1:]]
    return [0, 2, 4, 6], [block, exchanged(block, 2), exchanged(block, 4)]


def far_halves(pieces):
    if not paired():
        return []
    half = pieces[0].shape[0] // 2
    return [exchanged(pieces[1][:half], 4), exchanged(pieces[2][half:], 2)]


def with_far(pieces, halves):
    return pieces + [jnp.concatenate(halves, axis=0)] if halves else pieces


def butterfly_sum(values):
    for axis in ("grp", "rep"):
        count = lax.axis_size(axis)
        step = 1
        while step < count:
            route = [(i, i ^ step) for i in range(count)]
            values = values + lax.ppermute(values, axis, route)
            step *= 2
    return values


def stack_near(block):
    offsets = (2, 4, 6) if paired() else range(1, lax.axis_size("grp"))
    return [exchanged(block, k) for k in offsets]


def stack_all(block, near):
    near = jnp.stack([block, *near])
    return [near, exchanged(near, 1)] if paired() else [near]


def stack_offsets():
    return [0, 2, 4, 6, 1, 3, 5, 7] if paired() else list(range(lax.axis_size("grp")))


def rep_swap(block, step):
    count = lax.axis_size("rep")
    return lax.ppermute(block, "rep", [(i, i ^ step) for i in range(count)])


def rep_steps():
    count = lax.axis_size("rep")
    steps = [1 << bit for bit in range(count.bit_length() - 1)]
    return steps, steps[::-1]


def halves_of(blocks, step):
    bit = (lax.axis_index("rep") // step) % 2
    rows = blocks[0].shape[0] // 2

    def total(place):
        parts = [lax.dynamic_slice_in_dim(b, place * rows, rows, 0) for b in blocks]
        if len(parts) == 1:
            return parts[0]
        return sum(p.astype(F32) for p in parts).astype(BF)

    return total(bit), total(1 - bit)


def added(one, two):
    return (one.astype(F32) + two.astype(F32)).astype(BF)


def joined(block, other, step):
    bit = (lax.axis_index("rep") // step) % 2
    return jnp.where(
        bit == 0,
        jnp.concatenate([block, other], axis=0),
        jnp.concatenate([other, block], axis=0),
    )


class SumQueue:
    def __init__(self, orders, parts):
        self.parts = list(parts)
        self.order = orders[0]
        self.plans = [self.plan(order, 1) for order in orders]
        self.start()

    @staticmethod
    def plan(order, skipped):
        return [(step, True) for step in order][skipped:] + [(step, False) for step in order[::-1]]

    def start(self):
        self.moved, self.kept = [], []
        for place, plan in enumerate(self.plans):
            keep = send = self.parts[place]
            if plan and plan[0][1]:
                keep, send = halves_of([keep], plan[0][0])
            self.kept.append(keep)
            self.moved.append(rep_swap(send, plan[0][0]) if plan else None)

    def end(self):
        for place, plan in enumerate(self.plans):
            if plan:
                step, halving = plan.pop(0)
                merge = added if halving else functools.partial(joined, step=step)
                self.parts[place] = merge(self.kept[place], self.moved[place])

    def turn(self, value, late=None):
        value, self.moved = lax.optimization_barrier((value, self.moved))
        self.end()
        if late is not None:
            self.parts.append(late)
            self.plans.append(self.plan(self.order, 0))
        self.start()
        return value

    def finish(self):
        while any(self.plans):
            self.end()
            self.start()
        return self.parts


def body(
    tokens, seg_ids, valid_mask, norm_gain, conv_taps, mix_in, mix_out, ffn_gain, ffn_in, ffn_out,
    grad_out,
):
    row_count, model_width = tokens.shape
    mine = lax.axis_index("grp")
    qk_width = HEADS * FEAT
    v_width = HEADS * VDIM
    hidden = ffn_in.shape[0]

    full_in = lax.all_gather(mix_in, "grp", axis=0, tiled=True)
    full_out = lax.all_gather(mix_out, "grp", axis=0, tiled=True)
    if paired():
        w_in = jnp.concatenate([ffn_in, exchanged(ffn_in, 1)], axis=0)
        w_out = jnp.concatenate([ffn_out, exchanged(ffn_out, 1)], axis=0)
    else:
        w_in, w_out = ffn_in, ffn_out

    x_full = tokens.astype(F32)
    id_float = seg_ids.astype(F32)
    keep_rows = valid_mask.astype(F32)
    edge = jnp.concatenate([x_full[row_count - 2 :], id_float[row_count - 2 :, None]], axis=1)
    edge = passed_along(edge, "grp", 1)
    ext_x = jnp.concatenate([edge[:, :model_width], x_full], axis=0)
    ext_ids = jnp.concatenate([edge[:, model_width], id_float], axis=0)
    ext_scale = row_scale(ext_x)
    ext_unit = ext_x * ext_scale
    ext_norm = ext_unit * norm_gain
    normed = ext_norm[2:]
    unit_in = ext_unit[2:]
    scale_in = ext_scale[2:]
    same_one = (ext_ids[1 : row_count + 1] == id_float).astype(F32)[:, None]
    same_two = (ext_ids[:row_count] == id_float).astype(F32)[:, None]
    back_one = ext_norm[1 : row_count + 1] * same_one
    back_two = ext_norm[:row_count] * same_two
    conv_out = conv_taps[:, 0] * normed + conv_taps[:, 1] * back_one + conv_taps[:, 2] * back_two
    gated = jax.nn.silu(normed)
    mixed = (conv_out * gated).astype(BF)
    mixed, w_in, w_out = lax.optimization_barrier((mixed, w_in, w_out))

    positions = jnp.arange(row_count)
    allowed = (
        (positions[:, None] <= positions[None, :]) & (seg_ids[:, None] == seg_ids[None, :])
    ).astype(F32) * keep_rows[:, None]
    last_id = seg_ids[row_count - 1]
    own = ((seg_ids == last_id).astype(F32) * keep_rows)[None, :]
    left, right, key_scale, query_scale = feature_tables()
    left_low, right_low = jnp.asarray(left, BF), jnp.asarray(right, BF)
    left_t, right_t = jnp.asarray(left.T, BF), jnp.asarray(right.T, BF)
    key_scale, query_scale = jnp.asarray(key_scale), jnp.asarray(query_scale)

    def whole(*shape):
        return pl.BlockSpec(shape, lambda h: (0,) * len(shape))

    smem = pl.BlockSpec(memory_space=pltpu.SMEM)
    qk_spec = pl.BlockSpec((FEAT, row_count), lambda h: (h, 0))
    k_spec = pl.BlockSpec((FEAT, row_count), lambda h: (HEADS + h, 0))
    v_spec = pl.BlockSpec((VDIM, row_count), lambda h: (h, 0))
    row_spec = pl.BlockSpec((1, 1, row_count), lambda h: (h, 0, 0))
    state_spec = pl.BlockSpec((1, FROWS, LANES), lambda h: (h, 0, 0))

    def stack_spec(stack):
        return pl.BlockSpec((stack.shape[0], 1, FROWS, LANES), lambda h: (0, h, 0, 0))

    one_row = whole(1, row_count)
    square = whole(row_count, row_count)
    table = whole(FROWS, EXT)
    table_t = whole(EXT, FROWS)
    column = whole(FROWS, 1)
    grid = (HEADS,)
    v_low = jax.ShapeDtypeStruct((v_width, row_count), BF)
    v_wide = jax.ShapeDtypeStruct((v_width, row_count), F32)
    qk_low = jax.ShapeDtypeStruct((qk_width, row_count), BF)
    qk_wide = jax.ShapeDtypeStruct((qk_width, row_count), F32)
    head_rows = jax.ShapeDtypeStruct((HEADS, 1, row_count), F32)
    states_low = jax.ShapeDtypeStruct((HEADS, FROWS, LANES), BF)
    states_wide = jax.ShapeDtypeStruct((HEADS, FROWS, LANES), F32)

    qk = dot(full_in[:, : 2 * qk_width], mixed, 0, 1).astype(BF)
    values = dot(full_in[:, 2 * qk_width :], mixed, 0, 1).astype(BF)

    id_pieces = jnp.stack([last_id // 256, last_id % 256]).astype(F32)
    states = call(
        state_kernel, states_low, grid,
        [smem, k_spec, v_spec, one_row, table, table, column], state_spec,
        10**9, 4 * 10**6,
        id_pieces, qk, values, own, left_low, right_low, key_scale,
    )
    near_states = stack_near(states)
    num_local, den_local = call(
        local_kernel, (v_wide, head_rows), grid,
        [qk_spec, k_spec, v_spec, square], (v_spec, row_spec),
        15 * 10**9, 7 * 10**6,
        qk, qk, values, allowed,
    )
    num_local, den_local, near_states = lax.optimization_barrier(
        (num_local, den_local, near_states)
    )
    state_stacks = stack_all(states, near_states)
    late_dy, state_stacks[0] = lax.optimization_barrier((grad_out, state_stacks[0]))
    dy_pieces = gather_near(late_dy)[1]
    dy_far = far_halves(dy_pieces)
    sources = mine ^ jnp.array(stack_offsets(), jnp.int32)
    id_parts = jnp.concatenate(
        [stack[:, 0, 0, VDIM + 2 : VDIM + 4] for stack in state_stacks], axis=0
    ).astype(F32)
    source_ids = id_parts[:, 0] * 256.0 + id_parts[:, 1]
    before = jnp.sum(jnp.where(sources == mine - 1, source_ids, 0.0))
    before = jnp.where(mine > 0, before, -1.0)
    marks = ((sources < mine) & (source_ids == before)).astype(F32)
    cont = (id_float == before).astype(F32)[None, :]
    attended, output, denom, state_in = call(
        functools.partial(carried_kernel, len(state_stacks)),
        (v_low, v_wide, head_rows, states_wide), grid,
        [smem, *map(stack_spec, state_stacks),
         qk_spec, v_spec, row_spec, one_row, table, table, column],
        (v_spec, v_spec, row_spec, state_spec),
        2 * 10**9, 16 * 10**6,
        marks, *state_stacks,
        qk, num_local, den_local, cont, left_low, right_low, query_scale,
    )
    branch = dot(attended, full_out, 0, 0)
    residual = x_full + branch
    scale_mid = row_scale(residual)
    unit_mid = residual * scale_mid
    normed_mid = (unit_mid * ffn_gain).astype(BF)

    offsets, mid_pieces = gather_near(normed_mid)
    units = w_in.shape[0]
    tokens_low = jax.ShapeDtypeStruct((row_count, model_width), BF)
    tokens_wide = jax.ShapeDtypeStruct((row_count, model_width), F32)
    tokens_spec = whole(row_count, model_width)
    once = pl.Buffered(1)
    def ffn_piece(x_piece, dy_piece):
        return call(
            ffn_kernel,
            (
                jax.ShapeDtypeStruct((1, row_count, units), BF),
                jax.ShapeDtypeStruct((2, row_count, units), BF),
                tokens_low,
            ),
            (1,),
            [
                tokens_spec, tokens_spec,
                pl.BlockSpec((units, 2 * model_width), lambda i: (0, 0), pipeline_mode=once),
                pl.BlockSpec((units, model_width), lambda i: (0, 0), pipeline_mode=once),
            ],
            (whole(1, row_count, units), whole(2, row_count, units), tokens_spec),
            0, 0, x_piece, dy_piece, w_in, w_out,
        )

    first = ffn_piece(mid_pieces[0], dy_pieces[0])
    *first, near = lax.optimization_barrier((*first, tuple(mid_pieces[1:])))
    mid_pieces = [mid_pieces[0], *near]
    mid_far = far_halves(mid_pieces)
    done = [first] + [ffn_piece(x, dy) for x, dy in zip(mid_pieces[1:], dy_pieces[1:])]
    done[-1], mid_far, dy_far = lax.optimization_barrier((list(done[-1]), mid_far, dy_far))
    mid_pieces, dy_pieces = with_far(mid_pieces, mid_far), with_far(dy_pieces, dy_far)
    done += [ffn_piece(x, dy) for x, dy in zip(mid_pieces[len(done) :], dy_pieces[len(done) :])]
    acts, pres, backs = map(list, zip(*done))
    acts, pres, backs[-1] = lax.optimization_barrier((acts, pres, backs[-1]))

    def weight_grads(lefts, rights):
        kinds = lefts[0].shape[0]
        cut = 256
        cuts = model_width // cut
        count = len(lefts)
        return call(
            functools.partial(weight_grad_kernel, count),
            tuple(
                jax.ShapeDtypeStruct((hidden, kinds * model_width), BF)
                for _ in range(units // hidden)
            ),
            (kinds, cuts),
            [pl.BlockSpec((1, row_count, units), lambda m, j: (m, 0, 0))] * count
            + [pl.BlockSpec((row_count, cut), lambda m, j: (0, j))] * count,
            tuple(
                pl.BlockSpec((hidden, cut), lambda m, j: (0, m * cuts + j))
                for _ in range(units // hidden)
            ),
            0, 0, *lefts, *rights,
        )

    back_terms = [exchanged(b, k) for b, k in zip(backs[1:], offsets[1:])]
    in_parts = weight_grads(pres, mid_pieces)
    acts, in_parts, back_terms[:-1] = lax.optimization_barrier((acts, in_parts, back_terms[:-1]))
    out_parts = weight_grads(acts, dy_pieces)
    results = [dot(act[0], w_out, 1, 0).astype(BF) for act in acts]
    orders = rep_steps()
    sums = [
        halves_of([own_part, *(exchanged(g, 1) for g in rest)], order[0])
        for (own_part, *rest), order in zip((in_parts, out_parts), orders)
    ]
    back_terms, results, sums = lax.optimization_barrier((back_terms, results, sums))
    back_terms = [backs[0], *back_terms]
    kept = [keep for keep, _ in sums]
    moved = [rep_swap(send, order[0]) for (_, send), order in zip(sums, orders)]
    *results, last_result = results
    result_terms = [exchanged(r, k) for r, k in zip(results[1:], offsets[1:])]
    tile = row_count // 4
    tile_spec = pl.BlockSpec((tile, model_width), lambda i: (i, 0))
    gain_spec = whole(1, model_width)
    grad_mid, grad_branch, grad_ffn_gain = call(
        functools.partial(mid_grad_kernel, len(back_terms)),
        (tokens_wide, tokens_low, jax.ShapeDtypeStruct((1, model_width), F32)), (4,),
        [tile_spec] * (len(back_terms) + 2) + [gain_spec],
        (tile_spec, tile_spec, gain_spec),
        0, 0, *back_terms, residual, grad_out, ffn_gain[None],
    )
    grad_att = dot(full_out, grad_branch, 1, 1)
    state_grads, dnum, dden = call(
        state_grad_kernel, (states_low, v_low, head_rows), grid,
        [v_spec, v_spec, row_spec, qk_spec, one_row, table, table, column],
        (state_spec, v_spec, row_spec),
        2 * 10**9, 12 * 10**6,
        grad_att, output, denom, qk, cont, left_low, right_low, query_scale,
    )
    state_grads, result_terms = lax.optimization_barrier((state_grads, result_terms))
    near_grads = stack_near(state_grads)
    grad_queries, dk_local, dv_local = call(
        local_grad_kernel, (qk_low, qk_wide, v_wide), grid,
        [qk_spec, k_spec, v_spec, v_spec, row_spec, square, state_spec, one_row,
         table, table, table_t, table_t, column],
        (qk_spec, qk_spec, v_spec),
        30 * 10**9, 12 * 10**6,
        qk, qk, values, dnum, dden, allowed, state_in, cont,
        left_low, right_low, left_t, right_t, query_scale,
    )
    dk_local, dv_local, near_grads, moved = lax.optimization_barrier(
        (dk_local, dv_local, near_grads, moved)
    )
    grad_stacks = stack_all(state_grads, near_grads)
    queue = SumQueue(orders, [added(k, m) for k, m in zip(kept, moved)])
    late_attended, grad_stacks[0] = lax.optimization_barrier((attended, grad_stacks[0]))
    out_terms = dot(late_attended, grad_branch, 1, 0).astype(BF)
    out_shard = lax.psum_scatter(out_terms, "grp", scatter_dimension=0, tiled=True)
    earlier = sources[None, :] == sources[:, None] - 1
    previous_ids = jnp.sum(jnp.where(earlier, source_ids[None, :], 0.0), axis=1)
    late_marks = ((sources > mine) & (previous_ids == id_float[row_count - 1])).astype(F32)
    grad_keys, grad_values = call(
        functools.partial(late_grad_kernel, len(grad_stacks)), (qk_low, v_low), grid,
        [smem, *map(stack_spec, grad_stacks), k_spec, v_spec, one_row, qk_spec, v_spec,
         table, table, table_t, table_t, column],
        (qk_spec, v_spec),
        2 * 10**9, 14 * 10**6,
        late_marks, *grad_stacks, qk, values, own, dk_local, dv_local,
        left_low, right_low, left_t, right_t, key_scale,
    )
    grad_projected = jnp.concatenate([grad_queries, grad_keys, grad_values], axis=0)
    in_terms = dot(mixed, grad_projected, 0, 1).astype(BF)
    in_terms = queue.turn(in_terms)
    in_shard = lax.psum_scatter(in_terms, "grp", scatter_dimension=0, tiled=True)
    in_shard, last_result = lax.optimization_barrier((in_shard, last_result))
    grad_mix_in = lax.psum(in_shard, "rep").astype(F32)
    result_terms.append(exchanged(last_result, offsets[-1]))
    grad_mixed = dot(grad_projected, full_in, 0, 1)
    grad_mixed = queue.turn(grad_mixed, out_shard)
    edge_back = jnp.concatenate([grad_mixed[:2] * gated[:2], id_float[:2, None]], axis=1)
    edge_back = passed_along(edge_back, "grp", -1)
    ext_grad_ids = jnp.concatenate([id_float, edge_back[:, model_width]], axis=0)
    ahead_one = (ext_grad_ids[1 : row_count + 1] == id_float).astype(F32)[:, None]
    ahead_two = (ext_grad_ids[2:] == id_float).astype(F32)[:, None]
    flags = jnp.concatenate([same_one, same_two, ahead_one, ahead_two], axis=1)
    grad_tokens, sums = call(
        conv_grad_kernel, (tokens_low, jax.ShapeDtypeStruct((4, model_width), F32)), (1,),
        [
            tokens_spec, whole(2, model_width), whole(2, model_width), whole(row_count, 1),
            whole(row_count, 4), gain_spec, whole(3, model_width), tokens_spec, tokens_spec,
        ],
        (tokens_spec, whole(4, model_width)),
        0, 0,
        tokens, ext_norm[:2], edge_back[:, :model_width], scale_in, flags, norm_gain[None],
        conv_taps.T, grad_mixed, grad_mid,
        scratch=[pltpu.VMEM((row_count, model_width), F32)],
    )

    grad_tokens, sums = queue.turn((grad_tokens, sums))
    grad_ffn_in, grad_ffn_out, grad_mix_out = queue.finish()
    ffn_result = sum(term.astype(F32) for term in [results[0], *result_terms])
    mixed_out = (residual + ffn_result).astype(BF)

    stat_terms = jnp.stack(
        [
            jnp.sum(keep_rows * jnp.sum(x_full * x_full, axis=1)),
            jnp.sum(keep_rows * jnp.sum(branch * branch, axis=1)),
            jnp.sum(keep_rows * jnp.sum(ffn_result * ffn_result, axis=1)),
            jnp.sum(keep_rows),
        ]
    )
    small = jnp.concatenate([sums.reshape(-1), grad_ffn_gain[0], stat_terms])
    small = jnp.pad(small, (0, -small.shape[0] % 1024)).reshape(-1, LANES)
    small = butterfly_sum(small).reshape(-1)
    rows = small[: 5 * model_width].reshape(5, model_width)
    stats = small[5 * model_width : 5 * model_width + 4]
    layer_stats = jnp.sqrt(stats[:3] / (jnp.maximum(stats[3], 1.0) * model_width))
    return (
        mixed_out,
        grad_tokens,
        rows[0],
        rows[1:4].T,
        grad_mix_in,
        grad_mix_out.astype(F32),
        rows[4],
        grad_ffn_in.astype(F32),
        grad_ffn_out.astype(F32),
        layer_stats,
    )


def solution(mesh):
    split = P(("rep", "grp"), None)
    shard = P("grp", None)
    return jax.shard_map(
        body,
        mesh=mesh,
        in_specs=(
            split, P(("rep", "grp")), P(("rep", "grp")), P(), P(), shard, shard, P(), shard, shard,
            split,
        ),
        out_specs=(split, split, P(), P(), shard, shard, P(), shard, shard, P()),
        check_vma=False,
    )
```

```python
import functools
import math

import jax
import jax.numpy as jnp
import numpy as np
from jax import lax
from jax.experimental import pallas as pl
from jax.experimental.pallas import tpu as pltpu
from jax.sharding import PartitionSpec as P

HEADS = 16
FEAT = 16
VDIM = 112
PAIRS = FEAT * (FEAT + 1) // 2
FROWS = 160
LANES = 128
EXT = 32
EPSILON = 1e-05
OUTER_SCALE = 0.25 / math.sqrt(2.0)
BF = jnp.bfloat16
F32 = jnp.float32
VMEM_LIMIT = 50 * 1024 * 1024


def feature_tables():
    left = np.zeros((FROWS, EXT), np.float32)
    right = np.zeros((FROWS, EXT), np.float32)
    key_scale = np.zeros((FROWS, 1), np.float32)
    query_scale = np.zeros((FROWS, 1), np.float32)
    row = 0
    for i in range(FEAT):
        for j in range(i, FEAT):
            left[row, i] = 1.0
            right[row, j] = 1.0
            key_scale[row] = OUTER_SCALE
            query_scale[row] = OUTER_SCALE * (1.0 if i == j else 2.0)
            row += 1
    for i in range(FEAT):
        left[row, i] = 1.0
        right[row, FEAT] = 1.0
        key_scale[row] = query_scale[row] = 0.5
        row += 1
    left[row, FEAT] = right[row, FEAT] = 1.0
    key_scale[row] = query_scale[row] = 1.0
    return left, right, key_scale, query_scale


def dot(left, right, left_dim, right_dim):
    return lax.dot_general(
        left, right, (((left_dim,), (right_dim,)), ((), ())), preferred_element_type=F32
    )


def extended(vectors):
    rows = lax.broadcasted_iota(jnp.int32, (EXT - FEAT, vectors.shape[1]), 0)
    return jnp.concatenate([vectors, jnp.where(rows == 0, 1.0, 0.0).astype(BF)], axis=0)


def feature_parts(vectors, left, right):
    ext = extended(vectors)
    return dot(left, ext, 1, 0), dot(right, ext, 1, 0)


def padded_values(values):
    return jnp.concatenate(
        [values, jnp.zeros((LANES - VDIM, values.shape[1]), values.dtype)], axis=0
    )


def with_totals(state, total, high_id=None, low_id=None):
    lane = lax.broadcasted_iota(jnp.int32, state.shape, 1)
    high = total.astype(BF).astype(F32)
    out = jnp.where(lane == VDIM, high, state)
    out = jnp.where(lane == VDIM + 1, total - high, out)
    if high_id is not None:
        out = jnp.where(lane == VDIM + 2, high_id, out)
        out = jnp.where(lane == VDIM + 3, low_id, out)
    return out.astype(BF)


def total_of(state):
    lane = lax.broadcasted_iota(jnp.int32, state.shape, 1)
    return jnp.sum(
        jnp.where((lane == VDIM) | (lane == VDIM + 1), state, 0.0), axis=1, keepdims=True
    )


def state_kernel(ids_ref, keys_ref, values_ref, own_ref, left_ref, right_ref, scale_ref, out_ref):
    one, two = feature_parts(keys_ref[...], left_ref[...], right_ref[...])
    feats = one * two * scale_ref[...] * own_ref[...]
    state = dot(feats.astype(BF), padded_values(values_ref[...]), 1, 1)
    total = jnp.sum(feats, axis=1, keepdims=True)
    out_ref[0] = with_totals(state, total, ids_ref[0], ids_ref[1])


def tiles_of(count):
    half = count // 2
    return [(0, half, half), (half, count - half, count)]


def local_kernel(queries_ref, keys_ref, values_ref, allowed_ref, num_ref, den_ref):
    count = queries_ref.shape[1]
    for begin, width, seen in tiles_of(count):
        span = pl.ds(begin, width)
        scores = dot(keys_ref[:, :seen], queries_ref[:, span], 0, 0) * 0.25
        weights = (1.0 + scores + 0.5 * scores * scores) * allowed_ref[:seen, span]
        num_ref[:, span] = dot(values_ref[:, :seen], weights.astype(BF), 1, 0)
        den_ref[0, :, span] = jnp.sum(weights, axis=0, keepdims=True)


def marked_sum(marks_ref, gathered_refs):
    place = 0
    total = None
    for ref in gathered_refs:
        for slot in range(ref.shape[0]):
            term = ref[slot, 0].astype(F32) * marks_ref[place]
            total = term if total is None else total + term
            place += 1
    return total


def carried_kernel(stacks, marks_ref, *refs):
    gathered_refs = refs[:stacks]
    (queries_ref, num_ref, den_ref, cont_ref, left_ref, right_ref,
     scale_ref, attended_ref, output_ref, denom_ref, state_ref) = refs[stacks:]
    state = marked_sum(marks_ref, gathered_refs)
    state_ref[0] = state
    total = total_of(state)
    one, two = feature_parts(queries_ref[...], left_ref[...], right_ref[...])
    feats = one * two * scale_ref[...]
    cont = cont_ref[...]
    extra = dot(state.astype(BF), feats.astype(BF), 0, 0)[:VDIM]
    denom = den_ref[0] + cont * jnp.sum(feats * total, axis=0, keepdims=True)
    output = (num_ref[...] + cont * extra) / jnp.maximum(denom, 1.0)
    output_ref[...] = output
    attended_ref[...] = output.astype(BF)
    denom_ref[0] = denom


def state_grad_kernel(
    grad_ref, output_ref, denom_ref, queries_ref, cont_ref, left_ref, right_ref, scale_ref,
    out_ref, dnum_ref, dden_ref,
):
    denom = denom_ref[0]
    floor = jnp.maximum(denom, 1.0)
    grad = grad_ref[...]
    dnum = (grad / floor).astype(BF)
    dden = jnp.where(
        denom > 1.0, -jnp.sum(grad * output_ref[...], axis=0, keepdims=True) / floor, 0.0
    )
    dnum_ref[...] = dnum
    dden_ref[0] = dden
    cont = cont_ref[...]
    one, two = feature_parts(queries_ref[...], left_ref[...], right_ref[...])
    feats = one * two * scale_ref[...]
    state = dot(feats.astype(BF), padded_values(dnum * cont.astype(BF)), 1, 1)
    total = jnp.sum(feats * (cont * dden), axis=1, keepdims=True)
    out_ref[0] = with_totals(state, total)


def feature_back(grads, one, two, scale, left_t, right_t):
    scaled = grads * scale
    return (
        dot(left_t, (scaled * two).astype(BF), 1, 0) + dot(right_t, (scaled * one).astype(BF), 1, 0)
    )[:FEAT]


def local_grad_kernel(
    queries_ref, keys_ref, values_ref, dnum_ref, dden_ref, allowed_ref, state_ref, cont_ref,
    left_ref, right_ref, left_t_ref, right_t_ref, scale_ref, dq_ref, dk_ref, dv_ref,
):
    count = queries_ref.shape[1]
    state = state_ref[0]
    total = total_of(state)
    dnum = dnum_ref[...]
    one, two = feature_parts(queries_ref[...], left_ref[...], right_ref[...])
    grads = cont_ref[...] * (
        dot(state.astype(BF), padded_values(dnum), 1, 0) + total * dden_ref[0]
    )
    carried = feature_back(grads, one, two, scale_ref[...], left_t_ref[...], right_t_ref[...])
    for begin, width, seen in tiles_of(count):
        span = pl.ds(begin, width)
        keys = keys_ref[:, :seen]
        queries = queries_ref[:, span]
        scores = dot(keys, queries, 0, 0) * 0.25
        allowed = allowed_ref[:seen, span]
        weights = ((1.0 + scores + 0.5 * scores * scores) * allowed).astype(BF)
        dnum_part = dnum_ref[:, span]
        dweights = dot(values_ref[:, :seen], dnum_part, 0, 0) + dden_ref[0, :, span]
        dscores = (dweights * allowed * (1.0 + scores)).astype(BF)
        dq = dot(keys, dscores, 1, 0) * 0.25 + carried[:, begin : begin + width]
        dq_ref[:, span] = dq.astype(BF)
        dk = dot(queries, dscores, 1, 1) * 0.25
        dv = dot(dnum_part, weights, 1, 1)
        if begin == 0:
            dk_ref[:, :seen] = dk
            dv_ref[:, :seen] = dv
        else:
            dk_ref[:, :begin] += dk[:, :begin]
            dv_ref[:, :begin] += dv[:, :begin]
            dk_ref[:, span] = dk[:, begin:]
            dv_ref[:, span] = dv[:, begin:]


def late_grad_kernel(stacks, marks_ref, *refs):
    gathered_refs = refs[:stacks]
    (keys_ref, values_ref, own_ref, dk_in_ref, dv_in_ref, left_ref, right_ref, left_t_ref,
     right_t_ref, scale_ref, dk_ref, dv_ref) = refs[stacks:]
    state = marked_sum(marks_ref, gathered_refs)
    total = total_of(state)
    low = state.astype(BF)
    own = own_ref[...]
    one, two = feature_parts(keys_ref[...], left_ref[...], right_ref[...])
    feats = (one * two * scale_ref[...]).astype(BF)
    grads = own * (dot(low, padded_values(values_ref[...]), 1, 0) + total)
    back = feature_back(grads, one, two, scale_ref[...], left_t_ref[...], right_t_ref[...])
    dk_ref[...] = (dk_in_ref[...] + back).astype(BF)
    dv_ref[...] = (dv_in_ref[...] + own * dot(low, feats, 0, 0)[:VDIM]).astype(BF)


def ffn_kernel(x_ref, dy_ref, w_in_ref, w_out_ref, act_ref, pre_ref, back_ref):
    width = x_ref.shape[1]
    x = x_ref[...]
    gate = dot(x, w_in_ref[:, :width], 1, 1)
    up = dot(x, w_in_ref[:, width:], 1, 1)
    dact = dot(dy_ref[...], w_out_ref[...], 1, 1)
    sigma = 1.0 / (1.0 + jnp.exp(-gate))
    silu = gate * sigma
    act_ref[0] = (silu * up).astype(BF)
    dgate = (dact * up * (sigma * (1.0 + gate * (1.0 - sigma)))).astype(BF)
    dup = (dact * silu).astype(BF)
    pre_ref[0] = dgate
    pre_ref[1] = dup
    back_ref[...] = (
        dot(dgate, w_in_ref[:, :width], 1, 0) + dot(dup, w_in_ref[:, width:], 1, 0)
    ).astype(BF)


def weight_grad_kernel(pieces, *refs):
    lefts, rights, outs = refs[:pieces], refs[pieces : 2 * pieces], refs[2 * pieces :]
    total = None
    for left, right in zip(lefts, rights):
        term = dot(left[0], right[...], 0, 0)
        total = term if total is None else total + term
    rows = outs[0].shape[0]
    for place, out_ref in enumerate(outs):
        out_ref[...] = total[place * rows : (place + 1) * rows].astype(BF)


def product_kernel(left_dim, right_dim, left_ref, right_ref, out_ref):
    out_ref[...] = dot(left_ref[...], right_ref[...], left_dim, right_dim).astype(out_ref.dtype)


def mixed_grad_kernel(left_ref, right_ref, out_ref, turned_ref):
    @pl.when(pl.program_id(0) == 0)
    def _():
        turned_ref[...] = left_ref[...].T

    out_ref[...] = dot(turned_ref[...], right_ref[...], 1, 1)


def mid_grad_kernel(terms, *refs):
    term_refs = refs[:terms]
    residual_ref, grad_ref, gain_ref, mid_ref, branch_ref, gain_grad_ref = refs[terms:]
    grad = term_refs[0][...].astype(F32)
    for term_ref in term_refs[1:]:
        grad = grad + term_ref[...].astype(F32)
    residual = residual_ref[...]
    scale = lax.rsqrt(jnp.mean(residual * residual, axis=1, keepdims=True) + EPSILON)
    unit = residual * scale
    product = grad * unit
    part = jnp.sum(product, axis=0, keepdims=True)
    step = pl.program_id(0)

    @pl.when(step == 0)
    def _():
        gain_grad_ref[...] = part

    @pl.when(step > 0)
    def _():
        gain_grad_ref[...] += part

    gain = gain_ref[...]
    mean = jnp.mean(product * gain, axis=1, keepdims=True)
    mid = grad_ref[...].astype(F32) + scale * (grad * gain - unit * mean)
    mid_ref[...] = mid
    branch_ref[...] = mid.astype(BF)


def conv_grad_kernel(
    x_ref, before_ref, after_ref, scale_ref, flags_ref, gain_ref, taps_ref, mixed_ref, mid_ref,
    out_ref, sums_ref, scaled_ref,
):
    count, width = x_ref.shape
    cut = LANES
    row = lax.broadcasted_iota(jnp.int32, (count, cut), 0)

    def spread(column):
        return jnp.broadcast_to(column, (count, cut))

    scale = spread(scale_ref[...])
    same_one, same_two = spread(flags_ref[:, 0:1]), spread(flags_ref[:, 1:2])
    ahead_one, ahead_two = spread(flags_ref[:, 2:3]), spread(flags_ref[:, 3:4])

    def one_cut(index, total):
        span = pl.ds(pl.multiple_of(index * cut, cut), cut)
        gain = gain_ref[:, span]
        unit = x_ref[:, span].astype(F32) * scale
        normed = unit * gain
        older, newer = before_ref[0:1, span], before_ref[1:2, span]
        back_one = jnp.where(row == 0, newer, pltpu.roll(normed, 1, 0)) * same_one
        back_two = pltpu.roll(normed, 2, 0)
        back_two = jnp.where(row == 0, older, jnp.where(row == 1, newer, back_two)) * same_two
        tap_0, tap_1, tap_2 = taps_ref[0:1, span], taps_ref[1:2, span], taps_ref[2:3, span]
        conv = tap_0 * normed + tap_1 * back_one + tap_2 * back_two
        sigma = 1.0 / (1.0 + jnp.exp(-normed))
        mixed = mixed_ref[:, span]
        grad_conv = mixed * (normed * sigma)
        next_0, next_1 = after_ref[0:1, span], after_ref[1:2, span]
        on_one = jnp.where(row == count - 1, next_0, pltpu.roll(grad_conv, count - 1, 0))
        on_two = pltpu.roll(grad_conv, count - 2, 0)
        on_two = jnp.where(
            row == count - 2, next_0, jnp.where(row == count - 1, next_1, on_two)
        )
        grad = (
            mixed * conv * (sigma * (1.0 + normed * (1.0 - sigma)))
            + tap_0 * grad_conv
            + tap_1 * (on_one * ahead_one)
            + tap_2 * (on_two * ahead_two)
        )
        product = grad * unit
        sums_ref[0:1, span] = jnp.sum(product, axis=0, keepdims=True)
        sums_ref[1:2, span] = jnp.sum(grad_conv * normed, axis=0, keepdims=True)
        sums_ref[2:3, span] = jnp.sum(grad_conv * back_one, axis=0, keepdims=True)
        sums_ref[3:4, span] = jnp.sum(grad_conv * back_two, axis=0, keepdims=True)
        scaled_ref[:, span] = grad * gain
        return total + product * gain

    total = lax.fori_loop(0, width // cut, one_cut, jnp.zeros((count, cut), F32))
    mean = spread(jnp.sum(total, axis=1, keepdims=True) * (1.0 / width))

    def second(index, carry):
        span = pl.ds(pl.multiple_of(index * cut, cut), cut)
        unit = x_ref[:, span].astype(F32) * scale
        out_ref[:, span] = (mid_ref[:, span] + scale * (scaled_ref[:, span] - unit * mean)).astype(BF)
        return carry

    lax.fori_loop(0, width // cut, second, 0)


def call(kernel, outs, grid, in_specs, out_specs, flops, moved, *args, scratch=()):
    return pl.pallas_call(
        kernel,
        out_shape=outs,
        grid=grid,
        in_specs=in_specs,
        out_specs=out_specs,
        scratch_shapes=list(scratch),
        compiler_params=pltpu.CompilerParams(vmem_limit_bytes=VMEM_LIMIT),
        cost_estimate=pl.CostEstimate(flops=0, bytes_accessed=0, transcendentals=0),
    )(*args)


def passed_along(block, axis, distance):
    devices = range(lax.axis_size(axis))
    route = [(i - distance, i) for i in devices if i - distance in devices]
    return lax.ppermute(block, axis, route)


def silu_grad(values):
    sigma = jax.nn.sigmoid(values)
    return sigma * (1.0 + values * (1.0 - sigma))


def row_scale(values):
    return lax.rsqrt(jnp.mean(values * values, axis=-1, keepdims=True) + EPSILON)


def exchanged(block, offset):
    count = lax.axis_size("grp")
    return lax.ppermute(block, "grp", [(i, i ^ offset) for i in range(count)])


def paired():
    return lax.axis_size("grp") == 8


def gather_near(block):
    if not paired():
        offsets = list(range(lax.axis_size("grp")))
        return offsets, [block] + [exchanged(block, k) for k in offsets[1:]]
    return [0, 2, 4, 6], [block, exchanged(block, 2), exchanged(block, 4)]


def far_halves(pieces):
    if not paired():
        return []
    half = pieces[0].shape[0] // 2
    return [exchanged(pieces[1][:half], 4), exchanged(pieces[2][half:], 2)]


def with_far(pieces, halves):
    return pieces + [jnp.concatenate(halves, axis=0)] if halves else pieces


def butterfly_sum(values):
    for axis in ("grp", "rep"):
        count = lax.axis_size(axis)
        step = 1
        while step < count:
            route = [(i, i ^ step) for i in range(count)]
            values = values + lax.ppermute(values, axis, route)
            step *= 2
    return values


def stack_near(block):
    offsets = (2, 4, 6) if paired() else range(1, lax.axis_size("grp"))
    return [exchanged(block, k) for k in offsets]


def stack_all(block, near):
    near = jnp.stack([block, *near])
    return [near, exchanged(near, 1)] if paired() else [near]


def stack_offsets():
    return [0, 2, 4, 6, 1, 3, 5, 7] if paired() else list(range(lax.axis_size("grp")))


def rep_swap(block, step):
    count = lax.axis_size("rep")
    return lax.ppermute(block, "rep", [(i, i ^ step) for i in range(count)])


def rep_steps():
    count = lax.axis_size("rep")
    steps = [1 << bit for bit in range(count.bit_length() - 1)]
    return steps, steps[::-1]


def halves_of(blocks, step):
    bit = (lax.axis_index("rep") // step) % 2
    rows = blocks[0].shape[0] // 2

    def total(place):
        parts = [lax.dynamic_slice_in_dim(b, place * rows, rows, 0) for b in blocks]
        if len(parts) == 1:
            return parts[0]
        return sum(p.astype(F32) for p in parts).astype(BF)

    return total(bit), total(1 - bit)


def added(one, two):
    return (one.astype(F32) + two.astype(F32)).astype(BF)


def joined(block, other, step):
    bit = (lax.axis_index("rep") // step) % 2
    return jnp.where(
        bit == 0,
        jnp.concatenate([block, other], axis=0),
        jnp.concatenate([other, block], axis=0),
    )


def rep_cycled(block, shift):
    count = lax.axis_size("rep")
    return lax.ppermute(block, "rep", [(i, (i + shift) % count) for i in range(count)])


def rep_scattered(terms):
    count = lax.axis_size("rep")
    mine = lax.axis_index("rep")
    rows = terms.shape[0] // count

    def part(index):
        return lax.dynamic_slice_in_dim(terms, lax.rem(index, count) * rows, rows, 0)

    return [part(mine)] + [rep_cycled(part(mine + s), s) for s in range(1, count)]


def rep_gathered(block):
    count = lax.axis_size("rep")
    mine = lax.axis_index("rep")
    parts = [block] + [rep_cycled(block, s) for s in range(1, count)]
    return jnp.concatenate(
        [
            sum(
                jnp.where(lax.rem(mine - index + count, count) == s, part.astype(F32), 0.0)
                for s, part in enumerate(parts)
            )
            for index in range(count)
        ],
        axis=0,
    )


class SumQueue:
    def __init__(self, orders, parts):
        self.parts = list(parts)
        self.plans = [self.plan(order, 1) for order in orders]
        self.start()

    @staticmethod
    def plan(order, skipped):
        return [(step, True) for step in order][skipped:] + [(step, False) for step in order[::-1]]

    def start(self):
        self.moved, self.kept = [], []
        for place, plan in enumerate(self.plans):
            keep = send = self.parts[place]
            if plan and plan[0][1]:
                keep, send = halves_of([keep], plan[0][0])
            self.kept.append(keep)
            self.moved.append(rep_swap(send, plan[0][0]) if plan else None)

    def end(self):
        for place, plan in enumerate(self.plans):
            if plan:
                step, halving = plan.pop(0)
                merge = added if halving else functools.partial(joined, step=step)
                self.parts[place] = merge(self.kept[place], self.moved[place])

    def turn(self, value):
        value, self.moved = lax.optimization_barrier((value, self.moved))
        self.end()
        self.start()
        return value

    def finish(self):
        while any(self.plans):
            self.end()
            self.start()
        return self.parts


def body(
    tokens, seg_ids, valid_mask, norm_gain, conv_taps, mix_in, mix_out, ffn_gain, ffn_in, ffn_out,
    grad_out,
):
    row_count, model_width = tokens.shape
    mine = lax.axis_index("grp")
    qk_width = HEADS * FEAT
    v_width = HEADS * VDIM
    hidden = ffn_in.shape[0]

    full_in = lax.all_gather(mix_in, "grp", axis=0, tiled=True)
    full_out = lax.all_gather(mix_out, "grp", axis=0, tiled=True)
    if paired():
        w_in = jnp.concatenate([ffn_in, exchanged(ffn_in, 1)], axis=0)
        w_out = jnp.concatenate([ffn_out, exchanged(ffn_out, 1)], axis=0)
    else:
        w_in, w_out = ffn_in, ffn_out

    x_full = tokens.astype(F32)
    id_float = seg_ids.astype(F32)
    keep_rows = valid_mask.astype(F32)
    edge = jnp.concatenate([x_full[row_count - 2 :], id_float[row_count - 2 :, None]], axis=1)
    edge = passed_along(edge, "grp", 1)
    ext_x = jnp.concatenate([edge[:, :model_width], x_full], axis=0)
    ext_ids = jnp.concatenate([edge[:, model_width], id_float], axis=0)
    ext_scale = row_scale(ext_x)
    ext_unit = ext_x * ext_scale
    ext_norm = ext_unit * norm_gain
    normed = ext_norm[2:]
    unit_in = ext_unit[2:]
    scale_in = ext_scale[2:]
    same_one = (ext_ids[1 : row_count + 1] == id_float).astype(F32)[:, None]
    same_two = (ext_ids[:row_count] == id_float).astype(F32)[:, None]
    back_one = ext_norm[1 : row_count + 1] * same_one
    back_two = ext_norm[:row_count] * same_two
    conv_out = conv_taps[:, 0] * normed + conv_taps[:, 1] * back_one + conv_taps[:, 2] * back_two
    gated = jax.nn.silu(normed)
    mixed = (conv_out * gated).astype(BF)
    mixed, w_in, w_out = lax.optimization_barrier((mixed, w_in, w_out))

    positions = jnp.arange(row_count)
    allowed = (
        (positions[:, None] <= positions[None, :]) & (seg_ids[:, None] == seg_ids[None, :])
    ).astype(F32) * keep_rows[:, None]
    last_id = seg_ids[row_count - 1]
    own = ((seg_ids == last_id).astype(F32) * keep_rows)[None, :]
    left, right, key_scale, query_scale = feature_tables()
    left_low, right_low = jnp.asarray(left, BF), jnp.asarray(right, BF)
    left_t, right_t = jnp.asarray(left.T, BF), jnp.asarray(right.T, BF)
    key_scale, query_scale = jnp.asarray(key_scale), jnp.asarray(query_scale)

    def whole(*shape):
        return pl.BlockSpec(shape, lambda h: (0,) * len(shape))

    smem = pl.BlockSpec(memory_space=pltpu.SMEM)
    qk_spec = pl.BlockSpec((FEAT, row_count), lambda h: (h, 0))
    k_spec = pl.BlockSpec((FEAT, row_count), lambda h: (HEADS + h, 0))
    v_spec = pl.BlockSpec((VDIM, row_count), lambda h: (h, 0))
    row_spec = pl.BlockSpec((1, 1, row_count), lambda h: (h, 0, 0))
    state_spec = pl.BlockSpec((1, FROWS, LANES), lambda h: (h, 0, 0))

    def stack_spec(stack):
        return pl.BlockSpec((stack.shape[0], 1, FROWS, LANES), lambda h: (0, h, 0, 0))

    one_row = whole(1, row_count)
    square = whole(row_count, row_count)
    table = whole(FROWS, EXT)
    table_t = whole(EXT, FROWS)
    column = whole(FROWS, 1)
    grid = (HEADS,)
    v_low = jax.ShapeDtypeStruct((v_width, row_count), BF)
    v_wide = jax.ShapeDtypeStruct((v_width, row_count), F32)
    qk_low = jax.ShapeDtypeStruct((qk_width, row_count), BF)
    qk_wide = jax.ShapeDtypeStruct((qk_width, row_count), F32)
    head_rows = jax.ShapeDtypeStruct((HEADS, 1, row_count), F32)
    states_low = jax.ShapeDtypeStruct((HEADS, FROWS, LANES), BF)
    states_wide = jax.ShapeDtypeStruct((HEADS, FROWS, LANES), F32)

    qk = dot(full_in[:, : 2 * qk_width], mixed, 0, 1).astype(BF)
    values = dot(full_in[:, 2 * qk_width :], mixed, 0, 1).astype(BF)

    id_pieces = jnp.stack([last_id // 256, last_id % 256]).astype(F32)
    states = call(
        state_kernel, states_low, grid,
        [smem, k_spec, v_spec, one_row, table, table, column], state_spec,
        10**9, 4 * 10**6,
        id_pieces, qk, values, own, left_low, right_low, key_scale,
    )
    near_states = stack_near(states)
    num_local, den_local = call(
        local_kernel, (v_wide, head_rows), grid,
        [qk_spec, k_spec, v_spec, square], (v_spec, row_spec),
        15 * 10**9, 7 * 10**6,
        qk, qk, values, allowed,
    )
    num_local, den_local, near_states = lax.optimization_barrier(
        (num_local, den_local, near_states)
    )
    state_stacks = stack_all(states, near_states)
    late_dy, state_stacks[0] = lax.optimization_barrier((grad_out, state_stacks[0]))
    dy_pieces = gather_near(late_dy)[1]
    dy_far = far_halves(dy_pieces)
    sources = mine ^ jnp.array(stack_offsets(), jnp.int32)
    id_parts = jnp.concatenate(
        [stack[:, 0, 0, VDIM + 2 : VDIM + 4] for stack in state_stacks], axis=0
    ).astype(F32)
    source_ids = id_parts[:, 0] * 256.0 + id_parts[:, 1]
    before = jnp.sum(jnp.where(sources == mine - 1, source_ids, 0.0))
    before = jnp.where(mine > 0, before, -1.0)
    marks = ((sources < mine) & (source_ids == before)).astype(F32)
    cont = (id_float == before).astype(F32)[None, :]
    attended, output, denom, state_in = call(
        functools.partial(carried_kernel, len(state_stacks)),
        (v_low, v_wide, head_rows, states_wide), grid,
        [smem, *map(stack_spec, state_stacks),
         qk_spec, v_spec, row_spec, one_row, table, table, column],
        (v_spec, v_spec, row_spec, state_spec),
        2 * 10**9, 16 * 10**6,
        marks, *state_stacks,
        qk, num_local, den_local, cont, left_low, right_low, query_scale,
    )
    branch = dot(attended, full_out, 0, 0)
    residual = x_full + branch
    scale_mid = row_scale(residual)
    unit_mid = residual * scale_mid
    normed_mid = (unit_mid * ffn_gain).astype(BF)

    offsets, mid_pieces = gather_near(normed_mid)
    units = w_in.shape[0]
    tokens_low = jax.ShapeDtypeStruct((row_count, model_width), BF)
    tokens_wide = jax.ShapeDtypeStruct((row_count, model_width), F32)
    tokens_spec = whole(row_count, model_width)
    once = pl.Buffered(1)
    def ffn_piece(x_piece, dy_piece):
        return call(
            ffn_kernel,
            (
                jax.ShapeDtypeStruct((1, row_count, units), BF),
                jax.ShapeDtypeStruct((2, row_count, units), BF),
                tokens_low,
            ),
            (1,),
            [
                tokens_spec, tokens_spec,
                pl.BlockSpec((units, 2 * model_width), lambda i: (0, 0), pipeline_mode=once),
                pl.BlockSpec((units, model_width), lambda i: (0, 0), pipeline_mode=once),
            ],
            (whole(1, row_count, units), whole(2, row_count, units), tokens_spec),
            0, 0, x_piece, dy_piece, w_in, w_out,
        )

    first = ffn_piece(mid_pieces[0], dy_pieces[0])
    *first, near = lax.optimization_barrier((*first, tuple(mid_pieces[1:])))
    mid_pieces = [mid_pieces[0], *near]
    mid_far = far_halves(mid_pieces)
    done = [first] + [ffn_piece(x, dy) for x, dy in zip(mid_pieces[1:], dy_pieces[1:])]
    done[-1], mid_far, dy_far = lax.optimization_barrier((list(done[-1]), mid_far, dy_far))
    mid_pieces, dy_pieces = with_far(mid_pieces, mid_far), with_far(dy_pieces, dy_far)
    done += [ffn_piece(x, dy) for x, dy in zip(mid_pieces[len(done) :], dy_pieces[len(done) :])]
    acts, pres, backs = map(list, zip(*done))
    acts, pres, backs[-1] = lax.optimization_barrier((acts, pres, backs[-1]))

    def weight_grads(lefts, rights):
        kinds = lefts[0].shape[0]
        cut = 256
        cuts = model_width // cut
        count = len(lefts)
        return call(
            functools.partial(weight_grad_kernel, count),
            tuple(
                jax.ShapeDtypeStruct((hidden, kinds * model_width), BF)
                for _ in range(units // hidden)
            ),
            (kinds, cuts),
            [pl.BlockSpec((1, row_count, units), lambda m, j: (m, 0, 0))] * count
            + [pl.BlockSpec((row_count, cut), lambda m, j: (0, j))] * count,
            tuple(
                pl.BlockSpec((hidden, cut), lambda m, j: (0, m * cuts + j))
                for _ in range(units // hidden)
            ),
            0, 0, *lefts, *rights,
        )

    back_terms = [exchanged(b, k) for b, k in zip(backs[1:], offsets[1:])]
    in_parts = weight_grads(pres, mid_pieces)
    acts, in_parts, back_terms[:-1] = lax.optimization_barrier((acts, in_parts, back_terms[:-1]))
    out_parts = weight_grads(acts, dy_pieces)
    results = [dot(act[0], w_out, 1, 0).astype(BF) for act in acts]
    orders = rep_steps()
    sums = [
        halves_of([own_part, *(exchanged(g, 1) for g in rest)], order[0])
        for (own_part, *rest), order in zip((in_parts, out_parts), orders)
    ]
    back_terms, results, sums = lax.optimization_barrier((back_terms, results, sums))
    back_terms = [backs[0], *back_terms]
    kept = [keep for keep, _ in sums]
    moved = [rep_swap(send, order[0]) for (_, send), order in zip(sums, orders)]
    *results, last_result = results
    result_terms = [exchanged(r, k) for r, k in zip(results[1:], offsets[1:])]
    tile = row_count // 4
    tile_spec = pl.BlockSpec((tile, model_width), lambda i: (i, 0))
    gain_spec = whole(1, model_width)
    grad_mid, grad_branch, grad_ffn_gain = call(
        functools.partial(mid_grad_kernel, len(back_terms)),
        (tokens_wide, tokens_low, jax.ShapeDtypeStruct((1, model_width), F32)), (4,),
        [tile_spec] * (len(back_terms) + 2) + [gain_spec],
        (tile_spec, tile_spec, gain_spec),
        0, 0, *back_terms, residual, grad_out, ffn_gain[None],
    )
    block_rows = 256
    blocks = (v_width // block_rows,)
    rows_spec = pl.BlockSpec((block_rows, model_width), lambda i: (i, 0))
    columns_spec = pl.BlockSpec((block_rows, row_count), lambda i: (i, 0))
    grad_att = call(
        functools.partial(product_kernel, 1, 1), v_wide, blocks,
        [rows_spec, tokens_spec], columns_spec, 0, 0, full_out, grad_branch,
    )
    state_grads, dnum, dden = call(
        state_grad_kernel, (states_low, v_low, head_rows), grid,
        [v_spec, v_spec, row_spec, qk_spec, one_row, table, table, column],
        (state_spec, v_spec, row_spec),
        2 * 10**9, 12 * 10**6,
        grad_att, output, denom, qk, cont, left_low, right_low, query_scale,
    )
    state_grads, result_terms = lax.optimization_barrier((state_grads, result_terms))
    late_attended, state_grads = lax.optimization_barrier((attended, state_grads))
    near_grads = stack_near(state_grads)
    out_terms = call(
        functools.partial(product_kernel, 1, 0),
        jax.ShapeDtypeStruct((v_width, model_width), BF), blocks,
        [columns_spec, tokens_spec], rows_spec, 0, 0, late_attended, grad_branch,
    )
    dnum, out_terms, moved = lax.optimization_barrier((dnum, out_terms, moved))
    queue = SumQueue(orders, [added(k, m) for k, m in zip(kept, moved)])
    grad_queries, dk_local, dv_local = call(
        local_grad_kernel, (qk_low, qk_wide, v_wide), grid,
        [qk_spec, k_spec, v_spec, v_spec, row_spec, square, state_spec, one_row,
         table, table, table_t, table_t, column],
        (qk_spec, qk_spec, v_spec),
        30 * 10**9, 12 * 10**6,
        qk, qk, values, dnum, dden, allowed, state_in, cont,
        left_low, right_low, left_t, right_t, query_scale,
    )
    dk_local, dv_local, near_grads = lax.optimization_barrier((dk_local, dv_local, near_grads))
    grad_stacks = stack_all(state_grads, near_grads)
    last_result, out_terms, grad_stacks[0] = lax.optimization_barrier(
        (last_result, out_terms, grad_stacks[0])
    )
    result_terms.append(exchanged(last_result, offsets[-1]))
    out_shard = lax.psum_scatter(out_terms, "grp", scatter_dimension=0, tiled=True)
    earlier = sources[None, :] == sources[:, None] - 1
    previous_ids = jnp.sum(jnp.where(earlier, source_ids[None, :], 0.0), axis=1)
    late_marks = ((sources > mine) & (previous_ids == id_float[row_count - 1])).astype(F32)
    grad_keys, grad_values = call(
        functools.partial(late_grad_kernel, len(grad_stacks)), (qk_low, v_low), grid,
        [smem, *map(stack_spec, grad_stacks), k_spec, v_spec, one_row, qk_spec, v_spec,
         table, table, table_t, table_t, column],
        (qk_spec, v_spec),
        2 * 10**9, 14 * 10**6,
        late_marks, *grad_stacks, qk, values, own, dk_local, dv_local,
        left_low, right_low, left_t, right_t, key_scale,
    )
    grad_keys, grad_values = queue.turn((grad_keys, grad_values))
    grad_projected = jnp.concatenate([grad_queries, grad_keys, grad_values], axis=0)
    in_width = full_in.shape[1]
    in_terms = call(
        functools.partial(product_kernel, 0, 1),
        jax.ShapeDtypeStruct((model_width, in_width), BF), (model_width // block_rows,),
        [pl.BlockSpec((row_count, block_rows), lambda i: (0, i)), whole(in_width, row_count)],
        pl.BlockSpec((block_rows, in_width), lambda i: (i, 0)),
        0, 0, mixed, grad_projected,
    )
    in_terms, result_terms = queue.turn((in_terms, result_terms))
    grad_projected, queue.kept = lax.optimization_barrier((grad_projected, queue.kept))
    ffn_result = sum(term.astype(F32) for term in [results[0], *result_terms])
    mixed_out = (residual + ffn_result).astype(BF)
    sum_ffn = jnp.sum(keep_rows * jnp.sum(ffn_result * ffn_result, axis=1))
    mixed_out, sum_ffn, grad_projected = lax.optimization_barrier(
        (mixed_out, sum_ffn, grad_projected)
    )
    in_shard = lax.psum_scatter(in_terms, "grp", scatter_dimension=0, tiled=True)
    grad_mixed = call(
        mixed_grad_kernel, tokens_wide, (model_width // block_rows,),
        [
            whole(in_width, row_count),
            pl.BlockSpec((block_rows, in_width), lambda i: (i, 0)),
        ],
        pl.BlockSpec((row_count, block_rows), lambda i: (0, i)),
        0, 0, grad_projected, full_in,
        scratch=[pltpu.VMEM((row_count, in_width), BF)],
    )
    grad_mixed, out_shard = lax.optimization_barrier((grad_mixed, out_shard))
    out_parts = rep_scattered(out_shard)
    edge_back = jnp.concatenate([grad_mixed[:2] * gated[:2], id_float[:2, None]], axis=1)
    edge_back = passed_along(edge_back, "grp", -1)
    ext_grad_ids = jnp.concatenate([id_float, edge_back[:, model_width]], axis=0)
    ahead_one = (ext_grad_ids[1 : row_count + 1] == id_float).astype(F32)[:, None]
    ahead_two = (ext_grad_ids[2:] == id_float).astype(F32)[:, None]
    flags = jnp.concatenate([same_one, same_two, ahead_one, ahead_two], axis=1)
    grad_tokens, sums = call(
        conv_grad_kernel, (tokens_low, jax.ShapeDtypeStruct((4, model_width), F32)), (1,),
        [
            tokens_spec, whole(2, model_width), whole(2, model_width), whole(row_count, 1),
            whole(row_count, 4), gain_spec, whole(3, model_width), tokens_spec, tokens_spec,
        ],
        (tokens_spec, whole(4, model_width)),
        0, 0,
        tokens, ext_norm[:2], edge_back[:, :model_width], scale_in, flags, norm_gain[None],
        conv_taps.T, grad_mixed, grad_mid,
        scratch=[pltpu.VMEM((row_count, model_width), F32)],
    )

    grad_tokens, sums, out_parts = queue.turn((grad_tokens, sums, out_parts))
    grad_ffn_in, grad_ffn_out = queue.finish()
    in_shard, grad_tokens, sums = lax.optimization_barrier((in_shard, grad_tokens, sums))
    in_parts = rep_scattered(in_shard)

    stat_terms = jnp.stack(
        [
            jnp.sum(keep_rows * jnp.sum(x_full * x_full, axis=1)),
            jnp.sum(keep_rows * jnp.sum(branch * branch, axis=1)),
            sum_ffn,
            jnp.sum(keep_rows),
        ]
    )
    small = jnp.concatenate([sums.reshape(-1), grad_ffn_gain[0], stat_terms])
    small = jnp.pad(small, (0, -small.shape[0] % 1024)).reshape(-1, LANES)
    in_parts, small = lax.optimization_barrier((in_parts, butterfly_sum(small)))
    small = small.reshape(-1)
    grad_mix_in = rep_gathered(sum(p.astype(F32) for p in in_parts).astype(BF))
    grad_mix_out = rep_gathered(sum(p.astype(F32) for p in out_parts).astype(BF))
    rows = small[: 5 * model_width].reshape(5, model_width)
    stats = small[5 * model_width : 5 * model_width + 4]
    layer_stats = jnp.sqrt(stats[:3] / (jnp.maximum(stats[3], 1.0) * model_width))
    return (
        mixed_out,
        grad_tokens,
        rows[0],
        rows[1:4].T,
        grad_mix_in,
        grad_mix_out,
        rows[4],
        grad_ffn_in.astype(F32),
        grad_ffn_out.astype(F32),
        layer_stats,
    )


def solution(mesh):
    split = P(("rep", "grp"), None)
    shard = P("grp", None)
    return jax.shard_map(
        body,
        mesh=mesh,
        in_specs=(
            split, P(("rep", "grp")), P(("rep", "grp")), P(), P(), shard, shard, P(), shard, shard,
            split,
        ),
        out_specs=(split, split, P(), P(), shard, shard, P(), shard, shard, P()),
        check_vma=False,
    )
```

```python
import functools
import math

import jax
import jax.numpy as jnp
import numpy as np
from jax import lax
from jax.experimental import pallas as pl
from jax.experimental.pallas import tpu as pltpu
from jax.sharding import PartitionSpec as P

HEADS = 16
FEAT = 16
VDIM = 112
PAIRS = FEAT * (FEAT + 1) // 2
FROWS = 160
LANES = 128
EXT = 32
EPSILON = 1e-05
OUTER_SCALE = 0.25 / math.sqrt(2.0)
BF = jnp.bfloat16
F32 = jnp.float32
VMEM_LIMIT = 50 * 1024 * 1024


def feature_tables():
    left = np.zeros((FROWS, EXT), np.float32)
    right = np.zeros((FROWS, EXT), np.float32)
    key_scale = np.zeros((FROWS, 1), np.float32)
    query_scale = np.zeros((FROWS, 1), np.float32)
    row = 0
    for i in range(FEAT):
        for j in range(i, FEAT):
            left[row, i] = 1.0
            right[row, j] = 1.0
            key_scale[row] = OUTER_SCALE
            query_scale[row] = OUTER_SCALE * (1.0 if i == j else 2.0)
            row += 1
    for i in range(FEAT):
        left[row, i] = 1.0
        right[row, FEAT] = 1.0
        key_scale[row] = query_scale[row] = 0.5
        row += 1
    left[row, FEAT] = right[row, FEAT] = 1.0
    key_scale[row] = query_scale[row] = 1.0
    return left, right, key_scale, query_scale


def dot(left, right, left_dim, right_dim):
    return lax.dot_general(
        left, right, (((left_dim,), (right_dim,)), ((), ())), preferred_element_type=F32
    )


def extended(vectors):
    rows = lax.broadcasted_iota(jnp.int32, (EXT - FEAT, vectors.shape[1]), 0)
    return jnp.concatenate([vectors, jnp.where(rows == 0, 1.0, 0.0).astype(BF)], axis=0)


def feature_parts(vectors, left, right):
    ext = extended(vectors)
    return dot(left, ext, 1, 0), dot(right, ext, 1, 0)


def padded_values(values):
    return jnp.concatenate(
        [values, jnp.zeros((LANES - VDIM, values.shape[1]), values.dtype)], axis=0
    )


def with_totals(state, total, high_id=None, low_id=None):
    lane = lax.broadcasted_iota(jnp.int32, state.shape, 1)
    high = total.astype(BF).astype(F32)
    out = jnp.where(lane == VDIM, high, state)
    out = jnp.where(lane == VDIM + 1, total - high, out)
    if high_id is not None:
        out = jnp.where(lane == VDIM + 2, high_id, out)
        out = jnp.where(lane == VDIM + 3, low_id, out)
    return out.astype(BF)


def total_of(state):
    lane = lax.broadcasted_iota(jnp.int32, state.shape, 1)
    return jnp.sum(
        jnp.where((lane == VDIM) | (lane == VDIM + 1), state, 0.0), axis=1, keepdims=True
    )


def state_kernel(ids_ref, keys_ref, values_ref, own_ref, left_ref, right_ref, scale_ref, out_ref):
    one, two = feature_parts(keys_ref[...], left_ref[...], right_ref[...])
    feats = one * two * scale_ref[...] * own_ref[...]
    state = dot(feats.astype(BF), padded_values(values_ref[...]), 1, 1)
    total = jnp.sum(feats, axis=1, keepdims=True)
    out_ref[0] = with_totals(state, total, ids_ref[0], ids_ref[1])


def tiles_of(count):
    half = count // 2
    return [(0, half, half), (half, count - half, count)]


def local_kernel(queries_ref, keys_ref, values_ref, allowed_ref, num_ref, den_ref):
    count = queries_ref.shape[1]
    for begin, width, seen in tiles_of(count):
        span = pl.ds(begin, width)
        scores = dot(keys_ref[:, :seen], queries_ref[:, span], 0, 0) * 0.25
        weights = (1.0 + scores + 0.5 * scores * scores) * allowed_ref[:seen, span]
        num_ref[:, span] = dot(values_ref[:, :seen], weights.astype(BF), 1, 0)
        den_ref[0, :, span] = jnp.sum(weights, axis=0, keepdims=True)


def marked_sum(marks_ref, gathered_refs):
    place = 0
    total = None
    for ref in gathered_refs:
        for slot in range(ref.shape[0]):
            term = ref[slot, 0].astype(F32) * marks_ref[place]
            total = term if total is None else total + term
            place += 1
    return total


def carried_kernel(stacks, marks_ref, *refs):
    gathered_refs = refs[:stacks]
    (queries_ref, num_ref, den_ref, cont_ref, left_ref, right_ref,
     scale_ref, attended_ref, output_ref, denom_ref, state_ref) = refs[stacks:]
    state = marked_sum(marks_ref, gathered_refs)
    state_ref[0] = state
    total = total_of(state)
    one, two = feature_parts(queries_ref[...], left_ref[...], right_ref[...])
    feats = one * two * scale_ref[...]
    cont = cont_ref[...]
    extra = dot(state.astype(BF), feats.astype(BF), 0, 0)[:VDIM]
    denom = den_ref[0] + cont * jnp.sum(feats * total, axis=0, keepdims=True)
    output = (num_ref[...] + cont * extra) / jnp.maximum(denom, 1.0)
    output_ref[...] = output
    attended_ref[...] = output.astype(BF)
    denom_ref[0] = denom


def state_grad_kernel(
    grad_ref, output_ref, denom_ref, queries_ref, cont_ref, left_ref, right_ref, scale_ref,
    out_ref, dnum_ref, dden_ref,
):
    denom = denom_ref[0]
    floor = jnp.maximum(denom, 1.0)
    grad = grad_ref[...]
    dnum = (grad / floor).astype(BF)
    dden = jnp.where(
        denom > 1.0, -jnp.sum(grad * output_ref[...], axis=0, keepdims=True) / floor, 0.0
    )
    dnum_ref[...] = dnum
    dden_ref[0] = dden
    cont = cont_ref[...]
    one, two = feature_parts(queries_ref[...], left_ref[...], right_ref[...])
    feats = one * two * scale_ref[...]
    state = dot(feats.astype(BF), padded_values(dnum * cont.astype(BF)), 1, 1)
    total = jnp.sum(feats * (cont * dden), axis=1, keepdims=True)
    out_ref[0] = with_totals(state, total)


def feature_back(grads, one, two, scale, left_t, right_t):
    scaled = grads * scale
    return (
        dot(left_t, (scaled * two).astype(BF), 1, 0) + dot(right_t, (scaled * one).astype(BF), 1, 0)
    )[:FEAT]


def local_grad_kernel(
    queries_ref, keys_ref, values_ref, dnum_ref, dden_ref, allowed_ref, state_ref, cont_ref,
    left_ref, right_ref, left_t_ref, right_t_ref, scale_ref, dq_ref, dk_ref, dv_ref,
):
    count = queries_ref.shape[1]
    state = state_ref[0]
    total = total_of(state)
    dnum = dnum_ref[...]
    one, two = feature_parts(queries_ref[...], left_ref[...], right_ref[...])
    grads = cont_ref[...] * (
        dot(state.astype(BF), padded_values(dnum), 1, 0) + total * dden_ref[0]
    )
    carried = feature_back(grads, one, two, scale_ref[...], left_t_ref[...], right_t_ref[...])
    for begin, width, seen in tiles_of(count):
        span = pl.ds(begin, width)
        keys = keys_ref[:, :seen]
        queries = queries_ref[:, span]
        scores = dot(keys, queries, 0, 0) * 0.25
        allowed = allowed_ref[:seen, span]
        weights = ((1.0 + scores + 0.5 * scores * scores) * allowed).astype(BF)
        dnum_part = dnum_ref[:, span]
        dweights = dot(values_ref[:, :seen], dnum_part, 0, 0) + dden_ref[0, :, span]
        dscores = (dweights * allowed * (1.0 + scores)).astype(BF)
        dq = dot(keys, dscores, 1, 0) * 0.25 + carried[:, begin : begin + width]
        dq_ref[:, span] = dq.astype(BF)
        dk = dot(queries, dscores, 1, 1) * 0.25
        dv = dot(dnum_part, weights, 1, 1)
        if begin == 0:
            dk_ref[:, :seen] = dk
            dv_ref[:, :seen] = dv
        else:
            dk_ref[:, :begin] += dk[:, :begin]
            dv_ref[:, :begin] += dv[:, :begin]
            dk_ref[:, span] = dk[:, begin:]
            dv_ref[:, span] = dv[:, begin:]


def late_grad_kernel(stacks, marks_ref, *refs):
    gathered_refs = refs[:stacks]
    (keys_ref, values_ref, own_ref, dk_in_ref, dv_in_ref, left_ref, right_ref, left_t_ref,
     right_t_ref, scale_ref, dk_ref, dv_ref) = refs[stacks:]
    state = marked_sum(marks_ref, gathered_refs)
    total = total_of(state)
    low = state.astype(BF)
    own = own_ref[...]
    one, two = feature_parts(keys_ref[...], left_ref[...], right_ref[...])
    feats = (one * two * scale_ref[...]).astype(BF)
    grads = own * (dot(low, padded_values(values_ref[...]), 1, 0) + total)
    back = feature_back(grads, one, two, scale_ref[...], left_t_ref[...], right_t_ref[...])
    dk_ref[...] = (dk_in_ref[...] + back).astype(BF)
    dv_ref[...] = (dv_in_ref[...] + own * dot(low, feats, 0, 0)[:VDIM]).astype(BF)


def ffn_kernel(x_ref, dy_ref, w_in_ref, w_out_ref, act_ref, pre_ref, back_ref):
    width = x_ref.shape[1]
    x = x_ref[...]
    gate = dot(x, w_in_ref[:, :width], 1, 1)
    up = dot(x, w_in_ref[:, width:], 1, 1)
    dact = dot(dy_ref[...], w_out_ref[...], 1, 1)
    sigma = 1.0 / (1.0 + jnp.exp(-gate))
    silu = gate * sigma
    act_ref[0] = (silu * up).astype(BF)
    dgate = (dact * up * (sigma * (1.0 + gate * (1.0 - sigma)))).astype(BF)
    dup = (dact * silu).astype(BF)
    pre_ref[0] = dgate
    pre_ref[1] = dup
    back_ref[...] = (
        dot(dgate, w_in_ref[:, :width], 1, 0) + dot(dup, w_in_ref[:, width:], 1, 0)
    ).astype(BF)


def weight_grad_kernel(pieces, *refs):
    lefts, rights, outs = refs[:pieces], refs[pieces : 2 * pieces], refs[2 * pieces :]
    total = None
    for left, right in zip(lefts, rights):
        term = dot(left[0], right[...], 0, 0)
        total = term if total is None else total + term
    rows = outs[0].shape[0]
    for place, out_ref in enumerate(outs):
        out_ref[...] = total[place * rows : (place + 1) * rows].astype(BF)


def product_kernel(left_dim, right_dim, left_ref, right_ref, out_ref):
    out_ref[...] = dot(left_ref[...], right_ref[...], left_dim, right_dim).astype(out_ref.dtype)


def mixed_grad_kernel(left_ref, right_ref, out_ref, turned_ref):
    @pl.when(pl.program_id(0) == 0)
    def _():
        turned_ref[...] = left_ref[...].T

    out_ref[...] = dot(turned_ref[...], right_ref[...], 1, 1)


def mid_grad_kernel(terms, *refs):
    term_refs = refs[:terms]
    residual_ref, grad_ref, gain_ref, mid_ref, branch_ref, gain_grad_ref = refs[terms:]
    grad = term_refs[0][...].astype(F32)
    for term_ref in term_refs[1:]:
        grad = grad + term_ref[...].astype(F32)
    residual = residual_ref[...]
    scale = lax.rsqrt(jnp.mean(residual * residual, axis=1, keepdims=True) + EPSILON)
    unit = residual * scale
    product = grad * unit
    part = jnp.sum(product, axis=0, keepdims=True)
    step = pl.program_id(0)

    @pl.when(step == 0)
    def _():
        gain_grad_ref[...] = part

    @pl.when(step > 0)
    def _():
        gain_grad_ref[...] += part

    gain = gain_ref[...]
    mean = jnp.mean(product * gain, axis=1, keepdims=True)
    mid = grad_ref[...].astype(F32) + scale * (grad * gain - unit * mean)
    mid_ref[...] = mid
    branch_ref[...] = mid.astype(BF)


def conv_grad_kernel(
    x_ref, before_ref, after_ref, scale_ref, flags_ref, gain_ref, taps_ref, mixed_ref, mid_ref,
    out_ref, sums_ref, scaled_ref,
):
    count, width = x_ref.shape
    cut = LANES
    row = lax.broadcasted_iota(jnp.int32, (count, cut), 0)

    def spread(column):
        return jnp.broadcast_to(column, (count, cut))

    scale = spread(scale_ref[...])
    same_one, same_two = spread(flags_ref[:, 0:1]), spread(flags_ref[:, 1:2])
    ahead_one, ahead_two = spread(flags_ref[:, 2:3]), spread(flags_ref[:, 3:4])

    def one_cut(index, total):
        span = pl.ds(pl.multiple_of(index * cut, cut), cut)
        gain = gain_ref[:, span]
        unit = x_ref[:, span].astype(F32) * scale
        normed = unit * gain
        older, newer = before_ref[0:1, span], before_ref[1:2, span]
        back_one = jnp.where(row == 0, newer, pltpu.roll(normed, 1, 0)) * same_one
        back_two = pltpu.roll(normed, 2, 0)
        back_two = jnp.where(row == 0, older, jnp.where(row == 1, newer, back_two)) * same_two
        tap_0, tap_1, tap_2 = taps_ref[0:1, span], taps_ref[1:2, span], taps_ref[2:3, span]
        conv = tap_0 * normed + tap_1 * back_one + tap_2 * back_two
        sigma = 1.0 / (1.0 + jnp.exp(-normed))
        mixed = mixed_ref[:, span]
        grad_conv = mixed * (normed * sigma)
        next_0, next_1 = after_ref[0:1, span], after_ref[1:2, span]
        on_one = jnp.where(row == count - 1, next_0, pltpu.roll(grad_conv, count - 1, 0))
        on_two = pltpu.roll(grad_conv, count - 2, 0)
        on_two = jnp.where(
            row == count - 2, next_0, jnp.where(row == count - 1, next_1, on_two)
        )
        grad = (
            mixed * conv * (sigma * (1.0 + normed * (1.0 - sigma)))
            + tap_0 * grad_conv
            + tap_1 * (on_one * ahead_one)
            + tap_2 * (on_two * ahead_two)
        )
        product = grad * unit
        sums_ref[0:1, span] = jnp.sum(product, axis=0, keepdims=True)
        sums_ref[1:2, span] = jnp.sum(grad_conv * normed, axis=0, keepdims=True)
        sums_ref[2:3, span] = jnp.sum(grad_conv * back_one, axis=0, keepdims=True)
        sums_ref[3:4, span] = jnp.sum(grad_conv * back_two, axis=0, keepdims=True)
        scaled_ref[:, span] = grad * gain
        return total + product * gain

    total = lax.fori_loop(0, width // cut, one_cut, jnp.zeros((count, cut), F32))
    mean = spread(jnp.sum(total, axis=1, keepdims=True) * (1.0 / width))

    def second(index, carry):
        span = pl.ds(pl.multiple_of(index * cut, cut), cut)
        unit = x_ref[:, span].astype(F32) * scale
        out_ref[:, span] = (mid_ref[:, span] + scale * (scaled_ref[:, span] - unit * mean)).astype(BF)
        return carry

    lax.fori_loop(0, width // cut, second, 0)


def call(kernel, outs, grid, in_specs, out_specs, flops, moved, *args, scratch=()):
    return pl.pallas_call(
        kernel,
        out_shape=outs,
        grid=grid,
        in_specs=in_specs,
        out_specs=out_specs,
        scratch_shapes=list(scratch),
        compiler_params=pltpu.CompilerParams(vmem_limit_bytes=VMEM_LIMIT),
        cost_estimate=pl.CostEstimate(flops=0, bytes_accessed=0, transcendentals=0),
    )(*args)


def passed_along(block, axis, distance):
    devices = range(lax.axis_size(axis))
    route = [(i - distance, i) for i in devices if i - distance in devices]
    return lax.ppermute(block, axis, route)


def silu_grad(values):
    sigma = jax.nn.sigmoid(values)
    return sigma * (1.0 + values * (1.0 - sigma))


def row_scale(values):
    return lax.rsqrt(jnp.mean(values * values, axis=-1, keepdims=True) + EPSILON)


def exchanged(block, offset):
    count = lax.axis_size("grp")
    return lax.ppermute(block, "grp", [(i, i ^ offset) for i in range(count)])


def paired():
    return lax.axis_size("grp") == 8


def gather_near(block):
    if not paired():
        offsets = list(range(lax.axis_size("grp")))
        return offsets, [block] + [exchanged(block, k) for k in offsets[1:]]
    return [0, 2, 4, 6], [block, exchanged(block, 2), exchanged(block, 4)]


def far_halves(pieces):
    if not paired():
        return []
    half = pieces[0].shape[0] // 2
    return [exchanged(pieces[1][:half], 4), exchanged(pieces[2][half:], 2)]


def with_far(pieces, halves):
    return pieces + [jnp.concatenate(halves, axis=0)] if halves else pieces


def butterfly_sum(values):
    for axis in ("grp", "rep"):
        count = lax.axis_size(axis)
        step = 1
        while step < count:
            route = [(i, i ^ step) for i in range(count)]
            values = values + lax.ppermute(values, axis, route)
            step *= 2
    return values


def stack_near(block):
    offsets = (2, 4, 6) if paired() else range(1, lax.axis_size("grp"))
    return [exchanged(block, k) for k in offsets]


def stack_all(block, near):
    near = jnp.stack([block, *near])
    return [near, exchanged(near, 1)] if paired() else [near]


def stack_offsets():
    return [0, 2, 4, 6, 1, 3, 5, 7] if paired() else list(range(lax.axis_size("grp")))


def rep_swap(block, step):
    count = lax.axis_size("rep")
    return lax.ppermute(block, "rep", [(i, i ^ step) for i in range(count)])


def rep_steps():
    count = lax.axis_size("rep")
    steps = [1 << bit for bit in range(count.bit_length() - 1)]
    return steps, steps[::-1]


def halves_of(blocks, step):
    bit = (lax.axis_index("rep") // step) % 2
    rows = blocks[0].shape[0] // 2

    def total(place):
        parts = [lax.dynamic_slice_in_dim(b, place * rows, rows, 0) for b in blocks]
        if len(parts) == 1:
            return parts[0]
        return sum(p.astype(F32) for p in parts).astype(BF)

    return total(bit), total(1 - bit)


def added(one, two):
    return (one.astype(F32) + two.astype(F32)).astype(BF)


def joined(block, other, step):
    bit = (lax.axis_index("rep") // step) % 2
    return jnp.where(
        bit == 0,
        jnp.concatenate([block, other], axis=0),
        jnp.concatenate([other, block], axis=0),
    )


def rep_cycled(block, shift):
    count = lax.axis_size("rep")
    return lax.ppermute(block, "rep", [(i, (i + shift) % count) for i in range(count)])


def rep_scattered(terms):
    count = lax.axis_size("rep")
    mine = lax.axis_index("rep")
    rows = terms.shape[0] // count

    def part(index):
        return lax.dynamic_slice_in_dim(terms, lax.rem(index, count) * rows, rows, 0)

    return [part(mine)] + [rep_cycled(part(mine + s), s) for s in range(1, count)]


def rep_gathered(block):
    count = lax.axis_size("rep")
    mine = lax.axis_index("rep")
    parts = [block] + [rep_cycled(block, s) for s in range(1, count)]
    return jnp.concatenate(
        [
            sum(
                jnp.where(lax.rem(mine - index + count, count) == s, part.astype(F32), 0.0)
                for s, part in enumerate(parts)
            )
            for index in range(count)
        ],
        axis=0,
    )


class SumQueue:
    def __init__(self, orders, parts):
        self.parts = list(parts)
        self.plans = [self.plan(order, 1) for order in orders]
        self.start()

    @staticmethod
    def plan(order, skipped):
        return [(step, True) for step in order][skipped:] + [(step, False) for step in order[::-1]]

    def start(self):
        self.moved, self.kept = [], []
        for place, plan in enumerate(self.plans):
            keep = send = self.parts[place]
            if plan and plan[0][1]:
                keep, send = halves_of([keep], plan[0][0])
            self.kept.append(keep)
            self.moved.append(rep_swap(send, plan[0][0]) if plan else None)

    def end(self):
        for place, plan in enumerate(self.plans):
            if plan:
                step, halving = plan.pop(0)
                merge = added if halving else functools.partial(joined, step=step)
                self.parts[place] = merge(self.kept[place], self.moved[place])

    def turn(self, value):
        value, self.moved = lax.optimization_barrier((value, self.moved))
        self.end()
        self.start()
        return value

    def finish(self):
        while any(self.plans):
            self.end()
            self.start()
        return self.parts


def body(
    tokens, seg_ids, valid_mask, norm_gain, conv_taps, mix_in, mix_out, ffn_gain, ffn_in, ffn_out,
    grad_out,
):
    row_count, model_width = tokens.shape
    mine = lax.axis_index("grp")
    qk_width = HEADS * FEAT
    v_width = HEADS * VDIM
    hidden = ffn_in.shape[0]

    full_in = lax.all_gather(mix_in, "grp", axis=0, tiled=True)
    full_out = lax.all_gather(mix_out, "grp", axis=0, tiled=True)
    if paired():
        w_in = jnp.concatenate([ffn_in, exchanged(ffn_in, 1)], axis=0)
        w_out = jnp.concatenate([ffn_out, exchanged(ffn_out, 1)], axis=0)
    else:
        w_in, w_out = ffn_in, ffn_out

    x_full = tokens.astype(F32)
    id_float = seg_ids.astype(F32)
    keep_rows = valid_mask.astype(F32)
    edge = jnp.concatenate([x_full[row_count - 2 :], id_float[row_count - 2 :, None]], axis=1)
    edge = passed_along(edge, "grp", 1)
    ext_x = jnp.concatenate([edge[:, :model_width], x_full], axis=0)
    ext_ids = jnp.concatenate([edge[:, model_width], id_float], axis=0)
    ext_scale = row_scale(ext_x)
    ext_unit = ext_x * ext_scale
    ext_norm = ext_unit * norm_gain
    normed = ext_norm[2:]
    unit_in = ext_unit[2:]
    scale_in = ext_scale[2:]
    same_one = (ext_ids[1 : row_count + 1] == id_float).astype(F32)[:, None]
    same_two = (ext_ids[:row_count] == id_float).astype(F32)[:, None]
    back_one = ext_norm[1 : row_count + 1] * same_one
    back_two = ext_norm[:row_count] * same_two
    conv_out = conv_taps[:, 0] * normed + conv_taps[:, 1] * back_one + conv_taps[:, 2] * back_two
    gated = jax.nn.silu(normed)
    mixed = (conv_out * gated).astype(BF)
    mixed, w_in, w_out = lax.optimization_barrier((mixed, w_in, w_out))

    positions = jnp.arange(row_count)
    allowed = (
        (positions[:, None] <= positions[None, :]) & (seg_ids[:, None] == seg_ids[None, :])
    ).astype(F32) * keep_rows[:, None]
    last_id = seg_ids[row_count - 1]
    own = ((seg_ids == last_id).astype(F32) * keep_rows)[None, :]
    left, right, key_scale, query_scale = feature_tables()
    left_low, right_low = jnp.asarray(left, BF), jnp.asarray(right, BF)
    left_t, right_t = jnp.asarray(left.T, BF), jnp.asarray(right.T, BF)
    key_scale, query_scale = jnp.asarray(key_scale), jnp.asarray(query_scale)

    def whole(*shape):
        return pl.BlockSpec(shape, lambda h: (0,) * len(shape))

    smem = pl.BlockSpec(memory_space=pltpu.SMEM)
    qk_spec = pl.BlockSpec((FEAT, row_count), lambda h: (h, 0))
    k_spec = pl.BlockSpec((FEAT, row_count), lambda h: (HEADS + h, 0))
    v_spec = pl.BlockSpec((VDIM, row_count), lambda h: (h, 0))
    row_spec = pl.BlockSpec((1, 1, row_count), lambda h: (h, 0, 0))
    state_spec = pl.BlockSpec((1, FROWS, LANES), lambda h: (h, 0, 0))

    def stack_spec(stack):
        return pl.BlockSpec((stack.shape[0], 1, FROWS, LANES), lambda h: (0, h, 0, 0))

    one_row = whole(1, row_count)
    square = whole(row_count, row_count)
    table = whole(FROWS, EXT)
    table_t = whole(EXT, FROWS)
    column = whole(FROWS, 1)
    grid = (HEADS,)
    v_low = jax.ShapeDtypeStruct((v_width, row_count), BF)
    v_wide = jax.ShapeDtypeStruct((v_width, row_count), F32)
    qk_low = jax.ShapeDtypeStruct((qk_width, row_count), BF)
    qk_wide = jax.ShapeDtypeStruct((qk_width, row_count), F32)
    head_rows = jax.ShapeDtypeStruct((HEADS, 1, row_count), F32)
    states_low = jax.ShapeDtypeStruct((HEADS, FROWS, LANES), BF)
    states_wide = jax.ShapeDtypeStruct((HEADS, FROWS, LANES), F32)

    qk = dot(full_in[:, : 2 * qk_width], mixed, 0, 1).astype(BF)
    values = dot(full_in[:, 2 * qk_width :], mixed, 0, 1).astype(BF)

    id_pieces = jnp.stack([last_id // 256, last_id % 256]).astype(F32)
    states = call(
        state_kernel, states_low, grid,
        [smem, k_spec, v_spec, one_row, table, table, column], state_spec,
        10**9, 4 * 10**6,
        id_pieces, qk, values, own, left_low, right_low, key_scale,
    )
    near_states = stack_near(states)
    num_local, den_local = call(
        local_kernel, (v_wide, head_rows), grid,
        [qk_spec, k_spec, v_spec, square], (v_spec, row_spec),
        15 * 10**9, 7 * 10**6,
        qk, qk, values, allowed,
    )
    num_local, den_local, near_states = lax.optimization_barrier(
        (num_local, den_local, near_states)
    )
    state_stacks = stack_all(states, near_states)
    late_dy, state_stacks[0] = lax.optimization_barrier((grad_out, state_stacks[0]))
    dy_pieces = gather_near(late_dy)[1]
    dy_far = far_halves(dy_pieces)
    sources = mine ^ jnp.array(stack_offsets(), jnp.int32)
    id_parts = jnp.concatenate(
        [stack[:, 0, 0, VDIM + 2 : VDIM + 4] for stack in state_stacks], axis=0
    ).astype(F32)
    source_ids = id_parts[:, 0] * 256.0 + id_parts[:, 1]
    before = jnp.sum(jnp.where(sources == mine - 1, source_ids, 0.0))
    before = jnp.where(mine > 0, before, -1.0)
    marks = ((sources < mine) & (source_ids == before)).astype(F32)
    cont = (id_float == before).astype(F32)[None, :]
    attended, output, denom, state_in = call(
        functools.partial(carried_kernel, len(state_stacks)),
        (v_low, v_wide, head_rows, states_wide), grid,
        [smem, *map(stack_spec, state_stacks),
         qk_spec, v_spec, row_spec, one_row, table, table, column],
        (v_spec, v_spec, row_spec, state_spec),
        2 * 10**9, 16 * 10**6,
        marks, *state_stacks,
        qk, num_local, den_local, cont, left_low, right_low, query_scale,
    )
    branch = dot(attended, full_out, 0, 0)
    residual = x_full + branch
    scale_mid = row_scale(residual)
    unit_mid = residual * scale_mid
    normed_mid = (unit_mid * ffn_gain).astype(BF)

    offsets, mid_pieces = gather_near(normed_mid)
    units = w_in.shape[0]
    tokens_low = jax.ShapeDtypeStruct((row_count, model_width), BF)
    tokens_wide = jax.ShapeDtypeStruct((row_count, model_width), F32)
    tokens_spec = whole(row_count, model_width)
    once = pl.Buffered(1)
    def ffn_piece(x_piece, dy_piece):
        return call(
            ffn_kernel,
            (
                jax.ShapeDtypeStruct((1, row_count, units), BF),
                jax.ShapeDtypeStruct((2, row_count, units), BF),
                tokens_low,
            ),
            (1,),
            [
                tokens_spec, tokens_spec,
                pl.BlockSpec((units, 2 * model_width), lambda i: (0, 0), pipeline_mode=once),
                pl.BlockSpec((units, model_width), lambda i: (0, 0), pipeline_mode=once),
            ],
            (whole(1, row_count, units), whole(2, row_count, units), tokens_spec),
            0, 0, x_piece, dy_piece, w_in, w_out,
        )

    first = ffn_piece(mid_pieces[0], dy_pieces[0])
    *first, near = lax.optimization_barrier((*first, tuple(mid_pieces[1:])))
    mid_pieces = [mid_pieces[0], *near]
    mid_far = far_halves(mid_pieces)
    done = [first] + [ffn_piece(x, dy) for x, dy in zip(mid_pieces[1:], dy_pieces[1:])]
    done[-1], mid_far, dy_far = lax.optimization_barrier((list(done[-1]), mid_far, dy_far))
    mid_pieces, dy_pieces = with_far(mid_pieces, mid_far), with_far(dy_pieces, dy_far)
    done += [ffn_piece(x, dy) for x, dy in zip(mid_pieces[len(done) :], dy_pieces[len(done) :])]
    acts, pres, backs = map(list, zip(*done))
    acts, pres, backs[-1] = lax.optimization_barrier((acts, pres, backs[-1]))

    def weight_grads(lefts, rights):
        kinds = lefts[0].shape[0]
        cut = 256
        cuts = model_width // cut
        count = len(lefts)
        return call(
            functools.partial(weight_grad_kernel, count),
            tuple(
                jax.ShapeDtypeStruct((hidden, kinds * model_width), BF)
                for _ in range(units // hidden)
            ),
            (kinds, cuts),
            [pl.BlockSpec((1, row_count, units), lambda m, j: (m, 0, 0))] * count
            + [pl.BlockSpec((row_count, cut), lambda m, j: (0, j))] * count,
            tuple(
                pl.BlockSpec((hidden, cut), lambda m, j: (0, m * cuts + j))
                for _ in range(units // hidden)
            ),
            0, 0, *lefts, *rights,
        )

    back_terms = [exchanged(b, k) for b, k in zip(backs[1:], offsets[1:])]
    in_parts = weight_grads(pres, mid_pieces)
    acts, in_parts, back_terms[:-1] = lax.optimization_barrier((acts, in_parts, back_terms[:-1]))
    out_parts = weight_grads(acts, dy_pieces)
    results = [dot(act[0], w_out, 1, 0).astype(BF) for act in acts]
    orders = rep_steps()
    sums = [
        halves_of([own_part, *(exchanged(g, 1) for g in rest)], order[0])
        for (own_part, *rest), order in zip((in_parts, out_parts), orders)
    ]
    back_terms, results, sums = lax.optimization_barrier((back_terms, results, sums))
    back_terms = [backs[0], *back_terms]
    kept = [keep for keep, _ in sums]
    moved = [rep_swap(send, order[0]) for (_, send), order in zip(sums, orders)]
    *results, last_result = results
    result_terms = [exchanged(r, k) for r, k in zip(results[1:], offsets[1:])]
    tile = row_count // 4
    tile_spec = pl.BlockSpec((tile, model_width), lambda i: (i, 0))
    gain_spec = whole(1, model_width)
    grad_mid, grad_branch, grad_ffn_gain = call(
        functools.partial(mid_grad_kernel, len(back_terms)),
        (tokens_wide, tokens_low, jax.ShapeDtypeStruct((1, model_width), F32)), (4,),
        [tile_spec] * (len(back_terms) + 2) + [gain_spec],
        (tile_spec, tile_spec, gain_spec),
        0, 0, *back_terms, residual, grad_out, ffn_gain[None],
    )
    block_rows = 256
    blocks = (v_width // block_rows,)
    rows_spec = pl.BlockSpec((block_rows, model_width), lambda i: (i, 0))
    columns_spec = pl.BlockSpec((block_rows, row_count), lambda i: (i, 0))
    grad_att = call(
        functools.partial(product_kernel, 1, 1), v_wide, blocks,
        [rows_spec, tokens_spec], columns_spec, 0, 0, full_out, grad_branch,
    )
    state_grads, dnum, dden = call(
        state_grad_kernel, (states_low, v_low, head_rows), grid,
        [v_spec, v_spec, row_spec, qk_spec, one_row, table, table, column],
        (state_spec, v_spec, row_spec),
        2 * 10**9, 12 * 10**6,
        grad_att, output, denom, qk, cont, left_low, right_low, query_scale,
    )
    state_grads, result_terms = lax.optimization_barrier((state_grads, result_terms))
    late_attended, state_grads = lax.optimization_barrier((attended, state_grads))
    near_grads = stack_near(state_grads)
    out_terms = call(
        functools.partial(product_kernel, 1, 0),
        jax.ShapeDtypeStruct((v_width, model_width), BF), blocks,
        [columns_spec, tokens_spec], rows_spec, 0, 0, late_attended, grad_branch,
    )
    dnum, out_terms, moved = lax.optimization_barrier((dnum, out_terms, moved))
    queue = SumQueue(orders, [added(k, m) for k, m in zip(kept, moved)])
    grad_queries, dk_local, dv_local = call(
        local_grad_kernel, (qk_low, qk_wide, v_wide), grid,
        [qk_spec, k_spec, v_spec, v_spec, row_spec, square, state_spec, one_row,
         table, table, table_t, table_t, column],
        (qk_spec, qk_spec, v_spec),
        30 * 10**9, 12 * 10**6,
        qk, qk, values, dnum, dden, allowed, state_in, cont,
        left_low, right_low, left_t, right_t, query_scale,
    )
    dk_local, dv_local, near_grads = lax.optimization_barrier((dk_local, dv_local, near_grads))
    grad_stacks = stack_all(state_grads, near_grads)
    last_result, out_terms, grad_stacks[0] = lax.optimization_barrier(
        (last_result, out_terms, grad_stacks[0])
    )
    result_terms.append(exchanged(last_result, offsets[-1]))
    out_shard = lax.psum_scatter(out_terms, "grp", scatter_dimension=0, tiled=True)
    earlier = sources[None, :] == sources[:, None] - 1
    previous_ids = jnp.sum(jnp.where(earlier, source_ids[None, :], 0.0), axis=1)
    late_marks = ((sources > mine) & (previous_ids == id_float[row_count - 1])).astype(F32)
    grad_keys, grad_values = call(
        functools.partial(late_grad_kernel, len(grad_stacks)), (qk_low, v_low), grid,
        [smem, *map(stack_spec, grad_stacks), k_spec, v_spec, one_row, qk_spec, v_spec,
         table, table, table_t, table_t, column],
        (qk_spec, v_spec),
        2 * 10**9, 14 * 10**6,
        late_marks, *grad_stacks, qk, values, own, dk_local, dv_local,
        left_low, right_low, left_t, right_t, key_scale,
    )
    grad_keys, grad_values = queue.turn((grad_keys, grad_values))
    grad_projected = jnp.concatenate([grad_queries, grad_keys, grad_values], axis=0)
    in_width = full_in.shape[1]
    in_terms = call(
        functools.partial(product_kernel, 0, 1),
        jax.ShapeDtypeStruct((model_width, in_width), BF), (model_width // block_rows,),
        [pl.BlockSpec((row_count, block_rows), lambda i: (0, i)), whole(in_width, row_count)],
        pl.BlockSpec((block_rows, in_width), lambda i: (i, 0)),
        0, 0, mixed, grad_projected,
    )
    in_terms, result_terms = queue.turn((in_terms, result_terms))
    grad_projected, queue.kept = lax.optimization_barrier((grad_projected, queue.kept))
    ffn_result = sum(term.astype(F32) for term in [results[0], *result_terms])
    mixed_out = (residual + ffn_result).astype(BF)
    sum_ffn = jnp.sum(keep_rows * jnp.sum(ffn_result * ffn_result, axis=1))
    mixed_out, sum_ffn, grad_projected = lax.optimization_barrier(
        (mixed_out, sum_ffn, grad_projected)
    )
    in_shard = lax.psum_scatter(in_terms, "grp", scatter_dimension=0, tiled=True)
    grad_mixed = call(
        mixed_grad_kernel, tokens_wide, (model_width // block_rows,),
        [
            whole(in_width, row_count),
            pl.BlockSpec((block_rows, in_width), lambda i: (i, 0)),
        ],
        pl.BlockSpec((row_count, block_rows), lambda i: (0, i)),
        0, 0, grad_projected, full_in,
        scratch=[pltpu.VMEM((row_count, in_width), BF)],
    )
    grad_mixed, out_shard = lax.optimization_barrier((grad_mixed, out_shard))
    out_parts = rep_scattered(out_shard)
    edge_back = jnp.concatenate([grad_mixed[:2] * gated[:2], id_float[:2, None]], axis=1)
    edge_back = passed_along(edge_back, "grp", -1)
    ext_grad_ids = jnp.concatenate([id_float, edge_back[:, model_width]], axis=0)
    ahead_one = (ext_grad_ids[1 : row_count + 1] == id_float).astype(F32)[:, None]
    ahead_two = (ext_grad_ids[2:] == id_float).astype(F32)[:, None]
    flags = jnp.concatenate([same_one, same_two, ahead_one, ahead_two], axis=1)
    grad_tokens, sums = call(
        conv_grad_kernel, (tokens_low, jax.ShapeDtypeStruct((4, model_width), F32)), (1,),
        [
            tokens_spec, whole(2, model_width), whole(2, model_width), whole(row_count, 1),
            whole(row_count, 4), gain_spec, whole(3, model_width), tokens_spec, tokens_spec,
        ],
        (tokens_spec, whole(4, model_width)),
        0, 0,
        tokens, ext_norm[:2], edge_back[:, :model_width], scale_in, flags, norm_gain[None],
        conv_taps.T, grad_mixed, grad_mid,
        scratch=[pltpu.VMEM((row_count, model_width), F32)],
    )

    grad_tokens, sums, out_parts, queue.moved = lax.optimization_barrier(
        (grad_tokens, sums, out_parts, queue.moved)
    )
    in_shard, grad_tokens, sums = lax.optimization_barrier((in_shard, grad_tokens, sums))
    in_parts = rep_scattered(in_shard)

    stat_terms = jnp.stack(
        [
            jnp.sum(keep_rows * jnp.sum(x_full * x_full, axis=1)),
            jnp.sum(keep_rows * jnp.sum(branch * branch, axis=1)),
            sum_ffn,
            jnp.sum(keep_rows),
        ]
    )
    small = jnp.concatenate([sums.reshape(-1), grad_ffn_gain[0], stat_terms])
    small = jnp.pad(small, (0, -small.shape[0] % 1024)).reshape(-1, LANES)
    in_parts, small, queue.kept = lax.optimization_barrier(
        (in_parts, butterfly_sum(small), queue.kept)
    )
    grad_ffn_in, grad_ffn_out = queue.finish()
    small = small.reshape(-1)
    grad_mix_in = rep_gathered(sum(p.astype(F32) for p in in_parts).astype(BF))
    grad_mix_out = rep_gathered(sum(p.astype(F32) for p in out_parts).astype(BF))
    rows = small[: 5 * model_width].reshape(5, model_width)
    stats = small[5 * model_width : 5 * model_width + 4]
    layer_stats = jnp.sqrt(stats[:3] / (jnp.maximum(stats[3], 1.0) * model_width))
    return (
        mixed_out,
        grad_tokens,
        rows[0],
        rows[1:4].T,
        grad_mix_in,
        grad_mix_out,
        rows[4],
        grad_ffn_in.astype(F32),
        grad_ffn_out.astype(F32),
        layer_stats,
    )


def solution(mesh):
    split = P(("rep", "grp"), None)
    shard = P("grp", None)
    return jax.shard_map(
        body,
        mesh=mesh,
        in_specs=(
            split, P(("rep", "grp")), P(("rep", "grp")), P(), P(), shard, shard, P(), shard, shard,
            split,
        ),
        out_specs=(split, split, P(), P(), shard, shard, P(), shard, shard, P()),
        check_vma=False,
    )
```

```python
import functools
import math

import jax
import jax.numpy as jnp
import numpy as np
from jax import lax
from jax.experimental import pallas as pl
from jax.experimental.pallas import tpu as pltpu
from jax.sharding import PartitionSpec as P

HEADS = 16
FEAT = 16
VDIM = 112
PAIRS = FEAT * (FEAT + 1) // 2
FROWS = 160
LANES = 128
EXT = 32
EPSILON = 1e-05
OUTER_SCALE = 0.25 / math.sqrt(2.0)
BF = jnp.bfloat16
F32 = jnp.float32
VMEM_LIMIT = 50 * 1024 * 1024


def feature_tables():
    left = np.zeros((FROWS, EXT), np.float32)
    right = np.zeros((FROWS, EXT), np.float32)
    key_scale = np.zeros((FROWS, 1), np.float32)
    query_scale = np.zeros((FROWS, 1), np.float32)
    row = 0
    for i in range(FEAT):
        for j in range(i, FEAT):
            left[row, i] = 1.0
            right[row, j] = 1.0
            key_scale[row] = OUTER_SCALE
            query_scale[row] = OUTER_SCALE * (1.0 if i == j else 2.0)
            row += 1
    for i in range(FEAT):
        left[row, i] = 1.0
        right[row, FEAT] = 1.0
        key_scale[row] = query_scale[row] = 0.5
        row += 1
    left[row, FEAT] = right[row, FEAT] = 1.0
    key_scale[row] = query_scale[row] = 1.0
    return left, right, key_scale, query_scale


def dot(left, right, left_dim, right_dim):
    return lax.dot_general(
        left, right, (((left_dim,), (right_dim,)), ((), ())), preferred_element_type=F32
    )


def extended(vectors):
    rows = lax.broadcasted_iota(jnp.int32, (EXT - FEAT, vectors.shape[1]), 0)
    return jnp.concatenate([vectors, jnp.where(rows == 0, 1.0, 0.0).astype(BF)], axis=0)


def feature_parts(vectors, left, right):
    ext = extended(vectors)
    return dot(left, ext, 1, 0), dot(right, ext, 1, 0)


def padded_values(values):
    return jnp.concatenate(
        [values, jnp.zeros((LANES - VDIM, values.shape[1]), values.dtype)], axis=0
    )


def with_totals(state, total, high_id=None, low_id=None):
    lane = lax.broadcasted_iota(jnp.int32, state.shape, 1)
    high = total.astype(BF).astype(F32)
    out = jnp.where(lane == VDIM, high, state)
    out = jnp.where(lane == VDIM + 1, total - high, out)
    if high_id is not None:
        out = jnp.where(lane == VDIM + 2, high_id, out)
        out = jnp.where(lane == VDIM + 3, low_id, out)
    return out.astype(BF)


def total_of(state):
    lane = lax.broadcasted_iota(jnp.int32, state.shape, 1)
    return jnp.sum(
        jnp.where((lane == VDIM) | (lane == VDIM + 1), state, 0.0), axis=1, keepdims=True
    )


def state_kernel(ids_ref, keys_ref, values_ref, own_ref, left_ref, right_ref, scale_ref, out_ref):
    one, two = feature_parts(keys_ref[...], left_ref[...], right_ref[...])
    feats = one * two * scale_ref[...] * own_ref[...]
    state = dot(feats.astype(BF), padded_values(values_ref[...]), 1, 1)
    total = jnp.sum(feats, axis=1, keepdims=True)
    out_ref[0] = with_totals(state, total, ids_ref[0], ids_ref[1])


def tiles_of(count):
    half = count // 2
    return [(0, half, half), (half, count - half, count)]


def local_kernel(queries_ref, keys_ref, values_ref, allowed_ref, num_ref, den_ref):
    count = queries_ref.shape[1]
    for begin, width, seen in tiles_of(count):
        span = pl.ds(begin, width)
        scores = dot(keys_ref[:, :seen], queries_ref[:, span], 0, 0) * 0.25
        weights = (1.0 + scores + 0.5 * scores * scores) * allowed_ref[:seen, span]
        num_ref[:, span] = dot(values_ref[:, :seen], weights.astype(BF), 1, 0)
        den_ref[0, :, span] = jnp.sum(weights, axis=0, keepdims=True)


def marked_sum(marks_ref, gathered_refs):
    place = 0
    total = None
    for ref in gathered_refs:
        for slot in range(ref.shape[0]):
            term = ref[slot, 0].astype(F32) * marks_ref[place]
            total = term if total is None else total + term
            place += 1
    return total


def carried_kernel(stacks, marks_ref, *refs):
    gathered_refs = refs[:stacks]
    (queries_ref, num_ref, den_ref, cont_ref, left_ref, right_ref,
     scale_ref, attended_ref, output_ref, denom_ref, state_ref) = refs[stacks:]
    state = marked_sum(marks_ref, gathered_refs)
    state_ref[0] = state
    total = total_of(state)
    one, two = feature_parts(queries_ref[...], left_ref[...], right_ref[...])
    feats = one * two * scale_ref[...]
    cont = cont_ref[...]
    extra = dot(state.astype(BF), feats.astype(BF), 0, 0)[:VDIM]
    denom = den_ref[0] + cont * jnp.sum(feats * total, axis=0, keepdims=True)
    output = (num_ref[...] + cont * extra) / jnp.maximum(denom, 1.0)
    output_ref[...] = output
    attended_ref[...] = output.astype(BF)
    denom_ref[0] = denom


def state_grad_kernel(
    grad_ref, output_ref, denom_ref, queries_ref, cont_ref, left_ref, right_ref, scale_ref,
    out_ref, dnum_ref, dden_ref,
):
    denom = denom_ref[0]
    floor = jnp.maximum(denom, 1.0)
    grad = grad_ref[...]
    dnum = (grad / floor).astype(BF)
    dden = jnp.where(
        denom > 1.0, -jnp.sum(grad * output_ref[...], axis=0, keepdims=True) / floor, 0.0
    )
    dnum_ref[...] = dnum
    dden_ref[0] = dden
    cont = cont_ref[...]
    one, two = feature_parts(queries_ref[...], left_ref[...], right_ref[...])
    feats = one * two * scale_ref[...]
    state = dot(feats.astype(BF), padded_values(dnum * cont.astype(BF)), 1, 1)
    total = jnp.sum(feats * (cont * dden), axis=1, keepdims=True)
    out_ref[0] = with_totals(state, total)


def feature_back(grads, one, two, scale, left_t, right_t):
    scaled = grads * scale
    return (
        dot(left_t, (scaled * two).astype(BF), 1, 0) + dot(right_t, (scaled * one).astype(BF), 1, 0)
    )[:FEAT]


def local_grad_kernel(
    queries_ref, keys_ref, values_ref, dnum_ref, dden_ref, allowed_ref, state_ref, cont_ref,
    left_ref, right_ref, left_t_ref, right_t_ref, scale_ref, dq_ref, dk_ref, dv_ref,
):
    count = queries_ref.shape[1]
    state = state_ref[0]
    total = total_of(state)
    dnum = dnum_ref[...]
    one, two = feature_parts(queries_ref[...], left_ref[...], right_ref[...])
    grads = cont_ref[...] * (
        dot(state.astype(BF), padded_values(dnum), 1, 0) + total * dden_ref[0]
    )
    carried = feature_back(grads, one, two, scale_ref[...], left_t_ref[...], right_t_ref[...])
    for begin, width, seen in tiles_of(count):
        span = pl.ds(begin, width)
        keys = keys_ref[:, :seen]
        queries = queries_ref[:, span]
        scores = dot(keys, queries, 0, 0) * 0.25
        allowed = allowed_ref[:seen, span]
        weights = ((1.0 + scores + 0.5 * scores * scores) * allowed).astype(BF)
        dnum_part = dnum_ref[:, span]
        dweights = dot(values_ref[:, :seen], dnum_part, 0, 0) + dden_ref[0, :, span]
        dscores = (dweights * allowed * (1.0 + scores)).astype(BF)
        dq = dot(keys, dscores, 1, 0) * 0.25 + carried[:, begin : begin + width]
        dq_ref[:, span] = dq.astype(BF)
        dk = dot(queries, dscores, 1, 1) * 0.25
        dv = dot(dnum_part, weights, 1, 1)
        if begin == 0:
            dk_ref[:, :seen] = dk
            dv_ref[:, :seen] = dv
        else:
            dk_ref[:, :begin] += dk[:, :begin]
            dv_ref[:, :begin] += dv[:, :begin]
            dk_ref[:, span] = dk[:, begin:]
            dv_ref[:, span] = dv[:, begin:]


def late_grad_kernel(stacks, marks_ref, *refs):
    gathered_refs = refs[:stacks]
    (keys_ref, values_ref, own_ref, dk_in_ref, dv_in_ref, left_ref, right_ref, left_t_ref,
     right_t_ref, scale_ref, dk_ref, dv_ref) = refs[stacks:]
    state = marked_sum(marks_ref, gathered_refs)
    total = total_of(state)
    low = state.astype(BF)
    own = own_ref[...]
    one, two = feature_parts(keys_ref[...], left_ref[...], right_ref[...])
    feats = (one * two * scale_ref[...]).astype(BF)
    grads = own * (dot(low, padded_values(values_ref[...]), 1, 0) + total)
    back = feature_back(grads, one, two, scale_ref[...], left_t_ref[...], right_t_ref[...])
    dk_ref[...] = (dk_in_ref[...] + back).astype(BF)
    dv_ref[...] = (dv_in_ref[...] + own * dot(low, feats, 0, 0)[:VDIM]).astype(BF)


def ffn_kernel(x_ref, dy_ref, w_in_ref, w_out_ref, act_ref, pre_ref, back_ref):
    width = x_ref.shape[1]
    x = x_ref[...]
    gate = dot(x, w_in_ref[:, :width], 1, 1)
    up = dot(x, w_in_ref[:, width:], 1, 1)
    dact = dot(dy_ref[...], w_out_ref[...], 1, 1)
    sigma = 1.0 / (1.0 + jnp.exp(-gate))
    silu = gate * sigma
    act_ref[0] = (silu * up).astype(BF)
    dgate = (dact * up * (sigma * (1.0 + gate * (1.0 - sigma)))).astype(BF)
    dup = (dact * silu).astype(BF)
    pre_ref[0] = dgate
    pre_ref[1] = dup
    back_ref[...] = (
        dot(dgate, w_in_ref[:, :width], 1, 0) + dot(dup, w_in_ref[:, width:], 1, 0)
    ).astype(BF)


def weight_grad_kernel(pieces, *refs):
    lefts, rights, outs = refs[:pieces], refs[pieces : 2 * pieces], refs[2 * pieces :]
    total = None
    for left, right in zip(lefts, rights):
        term = dot(left[0], right[...], 0, 0)
        total = term if total is None else total + term
    rows = outs[0].shape[0]
    for place, out_ref in enumerate(outs):
        out_ref[...] = total[place * rows : (place + 1) * rows].astype(BF)


def product_kernel(left_dim, right_dim, left_ref, right_ref, out_ref):
    out_ref[...] = dot(left_ref[...], right_ref[...], left_dim, right_dim).astype(out_ref.dtype)


def mixed_grad_kernel(left_ref, right_ref, out_ref, turned_ref):
    @pl.when(pl.program_id(0) == 0)
    def _():
        turned_ref[...] = left_ref[...].T

    out_ref[...] = dot(turned_ref[...], right_ref[...], 1, 1)


def mid_grad_kernel(terms, *refs):
    term_refs = refs[:terms]
    residual_ref, grad_ref, gain_ref, mid_ref, branch_ref, gain_grad_ref = refs[terms:]
    grad = term_refs[0][...].astype(F32)
    for term_ref in term_refs[1:]:
        grad = grad + term_ref[...].astype(F32)
    residual = residual_ref[...]
    scale = lax.rsqrt(jnp.mean(residual * residual, axis=1, keepdims=True) + EPSILON)
    unit = residual * scale
    product = grad * unit
    part = jnp.sum(product, axis=0, keepdims=True)
    step = pl.program_id(0)

    @pl.when(step == 0)
    def _():
        gain_grad_ref[...] = part

    @pl.when(step > 0)
    def _():
        gain_grad_ref[...] += part

    gain = gain_ref[...]
    mean = jnp.mean(product * gain, axis=1, keepdims=True)
    mid = grad_ref[...].astype(F32) + scale * (grad * gain - unit * mean)
    mid_ref[...] = mid
    branch_ref[...] = mid.astype(BF)


def conv_grad_kernel(
    x_ref, before_ref, after_ref, scale_ref, flags_ref, gain_ref, taps_ref, mixed_ref, mid_ref,
    out_ref, sums_ref, scaled_ref,
):
    count, width = x_ref.shape
    cut = LANES
    row = lax.broadcasted_iota(jnp.int32, (count, cut), 0)

    def spread(column):
        return jnp.broadcast_to(column, (count, cut))

    scale = spread(scale_ref[...])
    same_one, same_two = spread(flags_ref[:, 0:1]), spread(flags_ref[:, 1:2])
    ahead_one, ahead_two = spread(flags_ref[:, 2:3]), spread(flags_ref[:, 3:4])

    def one_cut(index, total):
        span = pl.ds(pl.multiple_of(index * cut, cut), cut)
        gain = gain_ref[:, span]
        unit = x_ref[:, span].astype(F32) * scale
        normed = unit * gain
        older, newer = before_ref[0:1, span], before_ref[1:2, span]
        back_one = jnp.where(row == 0, newer, pltpu.roll(normed, 1, 0)) * same_one
        back_two = pltpu.roll(normed, 2, 0)
        back_two = jnp.where(row == 0, older, jnp.where(row == 1, newer, back_two)) * same_two
        tap_0, tap_1, tap_2 = taps_ref[0:1, span], taps_ref[1:2, span], taps_ref[2:3, span]
        conv = tap_0 * normed + tap_1 * back_one + tap_2 * back_two
        sigma = 1.0 / (1.0 + jnp.exp(-normed))
        mixed = mixed_ref[:, span]
        grad_conv = mixed * (normed * sigma)
        next_0, next_1 = after_ref[0:1, span], after_ref[1:2, span]
        on_one = jnp.where(row == count - 1, next_0, pltpu.roll(grad_conv, count - 1, 0))
        on_two = pltpu.roll(grad_conv, count - 2, 0)
        on_two = jnp.where(
            row == count - 2, next_0, jnp.where(row == count - 1, next_1, on_two)
        )
        grad = (
            mixed * conv * (sigma * (1.0 + normed * (1.0 - sigma)))
            + tap_0 * grad_conv
            + tap_1 * (on_one * ahead_one)
            + tap_2 * (on_two * ahead_two)
        )
        product = grad * unit
        sums_ref[0:1, span] = jnp.sum(product, axis=0, keepdims=True)
        sums_ref[1:2, span] = jnp.sum(grad_conv * normed, axis=0, keepdims=True)
        sums_ref[2:3, span] = jnp.sum(grad_conv * back_one, axis=0, keepdims=True)
        sums_ref[3:4, span] = jnp.sum(grad_conv * back_two, axis=0, keepdims=True)
        scaled_ref[:, span] = grad * gain
        return total + product * gain

    total = lax.fori_loop(0, width // cut, one_cut, jnp.zeros((count, cut), F32))
    mean = spread(jnp.sum(total, axis=1, keepdims=True) * (1.0 / width))

    def second(index, carry):
        span = pl.ds(pl.multiple_of(index * cut, cut), cut)
        unit = x_ref[:, span].astype(F32) * scale
        out_ref[:, span] = (mid_ref[:, span] + scale * (scaled_ref[:, span] - unit * mean)).astype(BF)
        return carry

    lax.fori_loop(0, width // cut, second, 0)


def call(kernel, outs, grid, in_specs, out_specs, flops, moved, *args, scratch=()):
    return pl.pallas_call(
        kernel,
        out_shape=outs,
        grid=grid,
        in_specs=in_specs,
        out_specs=out_specs,
        scratch_shapes=list(scratch),
        compiler_params=pltpu.CompilerParams(vmem_limit_bytes=VMEM_LIMIT),
        cost_estimate=pl.CostEstimate(flops=0, bytes_accessed=0, transcendentals=0),
    )(*args)


def passed_along(block, axis, distance):
    devices = range(lax.axis_size(axis))
    route = [(i - distance, i) for i in devices if i - distance in devices]
    return lax.ppermute(block, axis, route)


def silu_grad(values):
    sigma = jax.nn.sigmoid(values)
    return sigma * (1.0 + values * (1.0 - sigma))


def row_scale(values):
    return lax.rsqrt(jnp.mean(values * values, axis=-1, keepdims=True) + EPSILON)


def exchanged(block, offset):
    count = lax.axis_size("grp")
    return lax.ppermute(block, "grp", [(i, i ^ offset) for i in range(count)])


def paired():
    return lax.axis_size("grp") == 8


def gather_near(block):
    if not paired():
        offsets = list(range(lax.axis_size("grp")))
        return offsets, [block] + [exchanged(block, k) for k in offsets[1:]]
    return [0, 2, 4, 6], [block, exchanged(block, 2), exchanged(block, 4)]


def far_halves(pieces):
    if not paired():
        return []
    half = pieces[0].shape[0] // 2
    return [exchanged(pieces[1][:half], 4), exchanged(pieces[2][half:], 2)]


def with_far(pieces, halves):
    return pieces + [jnp.concatenate(halves, axis=0)] if halves else pieces


def butterfly_sum(values):
    for axis in ("grp", "rep"):
        count = lax.axis_size(axis)
        step = 1
        while step < count:
            route = [(i, i ^ step) for i in range(count)]
            values = values + lax.ppermute(values, axis, route)
            step *= 2
    return values


def stack_near(block):
    offsets = (2, 4, 6) if paired() else range(1, lax.axis_size("grp"))
    return [exchanged(block, k) for k in offsets]


def stack_all(block, near):
    near = jnp.stack([block, *near])
    return [near, exchanged(near, 1)] if paired() else [near]


def stack_offsets():
    return [0, 2, 4, 6, 1, 3, 5, 7] if paired() else list(range(lax.axis_size("grp")))


def rep_swap(block, step):
    count = lax.axis_size("rep")
    return lax.ppermute(block, "rep", [(i, i ^ step) for i in range(count)])


def rep_steps():
    count = lax.axis_size("rep")
    steps = [1 << bit for bit in range(count.bit_length() - 1)]
    return steps, steps[::-1]


def halves_of(blocks, step):
    bit = (lax.axis_index("rep") // step) % 2
    rows = blocks[0].shape[0] // 2

    def total(place):
        parts = [lax.dynamic_slice_in_dim(b, place * rows, rows, 0) for b in blocks]
        if len(parts) == 1:
            return parts[0]
        return sum(p.astype(F32) for p in parts).astype(BF)

    return total(bit), total(1 - bit)


def added(one, two):
    return (one.astype(F32) + two.astype(F32)).astype(BF)


def joined(block, other, step):
    bit = (lax.axis_index("rep") // step) % 2
    return jnp.where(
        bit == 0,
        jnp.concatenate([block, other], axis=0),
        jnp.concatenate([other, block], axis=0),
    )


def rep_cycled(block, shift):
    count = lax.axis_size("rep")
    return lax.ppermute(block, "rep", [(i, (i + shift) % count) for i in range(count)])


def rep_scattered(terms):
    count = lax.axis_size("rep")
    mine = lax.axis_index("rep")
    rows = terms.shape[0] // count

    def part(index):
        return lax.dynamic_slice_in_dim(terms, lax.rem(index, count) * rows, rows, 0)

    return [part(mine)] + [rep_cycled(part(mine + s), s) for s in range(1, count)]


def rep_gathered(block):
    count = lax.axis_size("rep")
    mine = lax.axis_index("rep")
    parts = [block] + [rep_cycled(block, s) for s in range(1, count)]
    return jnp.concatenate(
        [
            sum(
                jnp.where(lax.rem(mine - index + count, count) == s, part.astype(F32), 0.0)
                for s, part in enumerate(parts)
            )
            for index in range(count)
        ],
        axis=0,
    )


class SumQueue:
    def __init__(self, orders, parts):
        self.parts = list(parts)
        self.plans = [self.plan(order, 1) for order in orders]
        self.start()

    @staticmethod
    def plan(order, skipped):
        return [(step, True) for step in order][skipped:] + [(step, False) for step in order[::-1]]

    def start(self):
        self.moved, self.kept = [], []
        for place, plan in enumerate(self.plans):
            keep = send = self.parts[place]
            if plan and plan[0][1]:
                keep, send = halves_of([keep], plan[0][0])
            self.kept.append(keep)
            self.moved.append(rep_swap(send, plan[0][0]) if plan else None)

    def end(self):
        for place, plan in enumerate(self.plans):
            if plan:
                step, halving = plan.pop(0)
                merge = added if halving else functools.partial(joined, step=step)
                self.parts[place] = merge(self.kept[place], self.moved[place])

    def turn(self, value):
        value, self.moved = lax.optimization_barrier((value, self.moved))
        self.end()
        self.start()
        return value

    def finish(self):
        while any(self.plans):
            self.end()
            self.start()
        return self.parts


def body(
    tokens, seg_ids, valid_mask, norm_gain, conv_taps, mix_in, mix_out, ffn_gain, ffn_in, ffn_out,
    grad_out,
):
    row_count, model_width = tokens.shape
    mine = lax.axis_index("grp")
    qk_width = HEADS * FEAT
    v_width = HEADS * VDIM
    hidden = ffn_in.shape[0]

    full_in = lax.all_gather(mix_in, "grp", axis=0, tiled=True)
    full_out = lax.all_gather(mix_out, "grp", axis=0, tiled=True)
    if paired():
        w_in = jnp.concatenate([ffn_in, exchanged(ffn_in, 1)], axis=0)
        w_out = jnp.concatenate([ffn_out, exchanged(ffn_out, 1)], axis=0)
    else:
        w_in, w_out = ffn_in, ffn_out

    x_full = tokens.astype(F32)
    id_float = seg_ids.astype(F32)
    keep_rows = valid_mask.astype(F32)
    edge = jnp.concatenate([x_full[row_count - 2 :], id_float[row_count - 2 :, None]], axis=1)
    edge = passed_along(edge, "grp", 1)
    ext_x = jnp.concatenate([edge[:, :model_width], x_full], axis=0)
    ext_ids = jnp.concatenate([edge[:, model_width], id_float], axis=0)
    ext_scale = row_scale(ext_x)
    ext_unit = ext_x * ext_scale
    ext_norm = ext_unit * norm_gain
    normed = ext_norm[2:]
    unit_in = ext_unit[2:]
    scale_in = ext_scale[2:]
    same_one = (ext_ids[1 : row_count + 1] == id_float).astype(F32)[:, None]
    same_two = (ext_ids[:row_count] == id_float).astype(F32)[:, None]
    back_one = ext_norm[1 : row_count + 1] * same_one
    back_two = ext_norm[:row_count] * same_two
    conv_out = conv_taps[:, 0] * normed + conv_taps[:, 1] * back_one + conv_taps[:, 2] * back_two
    gated = jax.nn.silu(normed)
    mixed = (conv_out * gated).astype(BF)
    mixed, w_in, w_out = lax.optimization_barrier((mixed, w_in, w_out))

    positions = jnp.arange(row_count)
    allowed = (
        (positions[:, None] <= positions[None, :]) & (seg_ids[:, None] == seg_ids[None, :])
    ).astype(F32) * keep_rows[:, None]
    last_id = seg_ids[row_count - 1]
    own = ((seg_ids == last_id).astype(F32) * keep_rows)[None, :]
    left, right, key_scale, query_scale = feature_tables()
    left_low, right_low = jnp.asarray(left, BF), jnp.asarray(right, BF)
    left_t, right_t = jnp.asarray(left.T, BF), jnp.asarray(right.T, BF)
    key_scale, query_scale = jnp.asarray(key_scale), jnp.asarray(query_scale)

    def whole(*shape):
        return pl.BlockSpec(shape, lambda h: (0,) * len(shape))

    smem = pl.BlockSpec(memory_space=pltpu.SMEM)
    qk_spec = pl.BlockSpec((FEAT, row_count), lambda h: (h, 0))
    k_spec = pl.BlockSpec((FEAT, row_count), lambda h: (HEADS + h, 0))
    v_spec = pl.BlockSpec((VDIM, row_count), lambda h: (h, 0))
    row_spec = pl.BlockSpec((1, 1, row_count), lambda h: (h, 0, 0))
    state_spec = pl.BlockSpec((1, FROWS, LANES), lambda h: (h, 0, 0))

    def stack_spec(stack):
        return pl.BlockSpec((stack.shape[0], 1, FROWS, LANES), lambda h: (0, h, 0, 0))

    one_row = whole(1, row_count)
    square = whole(row_count, row_count)
    table = whole(FROWS, EXT)
    table_t = whole(EXT, FROWS)
    column = whole(FROWS, 1)
    grid = (HEADS,)
    v_low = jax.ShapeDtypeStruct((v_width, row_count), BF)
    v_wide = jax.ShapeDtypeStruct((v_width, row_count), F32)
    qk_low = jax.ShapeDtypeStruct((qk_width, row_count), BF)
    qk_wide = jax.ShapeDtypeStruct((qk_width, row_count), F32)
    head_rows = jax.ShapeDtypeStruct((HEADS, 1, row_count), F32)
    states_low = jax.ShapeDtypeStruct((HEADS, FROWS, LANES), BF)
    states_wide = jax.ShapeDtypeStruct((HEADS, FROWS, LANES), F32)

    qk = dot(full_in[:, : 2 * qk_width], mixed, 0, 1).astype(BF)
    values = dot(full_in[:, 2 * qk_width :], mixed, 0, 1).astype(BF)

    id_pieces = jnp.stack([last_id // 256, last_id % 256]).astype(F32)
    states = call(
        state_kernel, states_low, grid,
        [smem, k_spec, v_spec, one_row, table, table, column], state_spec,
        10**9, 4 * 10**6,
        id_pieces, qk, values, own, left_low, right_low, key_scale,
    )
    near_states = stack_near(states)
    num_local, den_local = call(
        local_kernel, (v_wide, head_rows), grid,
        [qk_spec, k_spec, v_spec, square], (v_spec, row_spec),
        15 * 10**9, 7 * 10**6,
        qk, qk, values, allowed,
    )
    num_local, den_local, near_states = lax.optimization_barrier(
        (num_local, den_local, near_states)
    )
    state_stacks = stack_all(states, near_states)
    late_dy, state_stacks[0] = lax.optimization_barrier((grad_out, state_stacks[0]))
    dy_pieces = gather_near(late_dy)[1]
    dy_far = far_halves(dy_pieces)
    sources = mine ^ jnp.array(stack_offsets(), jnp.int32)
    id_parts = jnp.concatenate(
        [stack[:, 0, 0, VDIM + 2 : VDIM + 4] for stack in state_stacks], axis=0
    ).astype(F32)
    source_ids = id_parts[:, 0] * 256.0 + id_parts[:, 1]
    before = jnp.sum(jnp.where(sources == mine - 1, source_ids, 0.0))
    before = jnp.where(mine > 0, before, -1.0)
    marks = ((sources < mine) & (source_ids == before)).astype(F32)
    cont = (id_float == before).astype(F32)[None, :]
    attended, output, denom, state_in = call(
        functools.partial(carried_kernel, len(state_stacks)),
        (v_low, v_wide, head_rows, states_wide), grid,
        [smem, *map(stack_spec, state_stacks),
         qk_spec, v_spec, row_spec, one_row, table, table, column],
        (v_spec, v_spec, row_spec, state_spec),
        2 * 10**9, 16 * 10**6,
        marks, *state_stacks,
        qk, num_local, den_local, cont, left_low, right_low, query_scale,
    )
    branch = dot(attended, full_out, 0, 0)
    residual = x_full + branch
    scale_mid = row_scale(residual)
    unit_mid = residual * scale_mid
    normed_mid = (unit_mid * ffn_gain).astype(BF)

    offsets, mid_pieces = gather_near(normed_mid)
    units = w_in.shape[0]
    tokens_low = jax.ShapeDtypeStruct((row_count, model_width), BF)
    tokens_wide = jax.ShapeDtypeStruct((row_count, model_width), F32)
    tokens_spec = whole(row_count, model_width)
    once = pl.Buffered(1)
    def ffn_piece(x_piece, dy_piece):
        return call(
            ffn_kernel,
            (
                jax.ShapeDtypeStruct((1, row_count, units), BF),
                jax.ShapeDtypeStruct((2, row_count, units), BF),
                tokens_low,
            ),
            (1,),
            [
                tokens_spec, tokens_spec,
                pl.BlockSpec((units, 2 * model_width), lambda i: (0, 0), pipeline_mode=once),
                pl.BlockSpec((units, model_width), lambda i: (0, 0), pipeline_mode=once),
            ],
            (whole(1, row_count, units), whole(2, row_count, units), tokens_spec),
            0, 0, x_piece, dy_piece, w_in, w_out,
        )

    first = ffn_piece(mid_pieces[0], dy_pieces[0])
    *first, near = lax.optimization_barrier((*first, tuple(mid_pieces[1:])))
    mid_pieces = [mid_pieces[0], *near]
    mid_far = far_halves(mid_pieces)
    done = [first] + [ffn_piece(x, dy) for x, dy in zip(mid_pieces[1:], dy_pieces[1:])]
    done[-1], mid_far, dy_far = lax.optimization_barrier((list(done[-1]), mid_far, dy_far))
    mid_pieces, dy_pieces = with_far(mid_pieces, mid_far), with_far(dy_pieces, dy_far)
    done += [ffn_piece(x, dy) for x, dy in zip(mid_pieces[len(done) :], dy_pieces[len(done) :])]
    acts, pres, backs = map(list, zip(*done))
    acts, pres, backs[-1] = lax.optimization_barrier((acts, pres, backs[-1]))

    def weight_grads(lefts, rights):
        kinds = lefts[0].shape[0]
        cut = 256
        cuts = model_width // cut
        count = len(lefts)
        return call(
            functools.partial(weight_grad_kernel, count),
            tuple(
                jax.ShapeDtypeStruct((hidden, kinds * model_width), BF)
                for _ in range(units // hidden)
            ),
            (kinds, cuts),
            [pl.BlockSpec((1, row_count, units), lambda m, j: (m, 0, 0))] * count
            + [pl.BlockSpec((row_count, cut), lambda m, j: (0, j))] * count,
            tuple(
                pl.BlockSpec((hidden, cut), lambda m, j: (0, m * cuts + j))
                for _ in range(units // hidden)
            ),
            0, 0, *lefts, *rights,
        )

    back_terms = [exchanged(b, k) for b, k in zip(backs[1:], offsets[1:])]
    in_parts = weight_grads(pres, mid_pieces)
    acts, in_parts, back_terms[:-1] = lax.optimization_barrier((acts, in_parts, back_terms[:-1]))
    out_parts = weight_grads(acts, dy_pieces)
    results = [dot(act[0], w_out, 1, 0).astype(BF) for act in acts]
    orders = rep_steps()
    sums = [
        halves_of([own_part, *(exchanged(g, 1) for g in rest)], order[0])
        for (own_part, *rest), order in zip((in_parts, out_parts), orders)
    ]
    back_terms, results, sums = lax.optimization_barrier((back_terms, results, sums))
    back_terms = [backs[0], *back_terms]
    kept = [keep for keep, _ in sums]
    moved = [rep_swap(send, order[0]) for (_, send), order in zip(sums, orders)]
    *results, last_result = results
    result_terms = [exchanged(r, k) for r, k in zip(results[1:], offsets[1:])]
    tile = row_count // 4
    tile_spec = pl.BlockSpec((tile, model_width), lambda i: (i, 0))
    gain_spec = whole(1, model_width)
    grad_mid, grad_branch, grad_ffn_gain = call(
        functools.partial(mid_grad_kernel, len(back_terms)),
        (tokens_wide, tokens_low, jax.ShapeDtypeStruct((1, model_width), F32)), (4,),
        [tile_spec] * (len(back_terms) + 2) + [gain_spec],
        (tile_spec, tile_spec, gain_spec),
        0, 0, *back_terms, residual, grad_out, ffn_gain[None],
    )
    block_rows = 256
    blocks = (v_width // block_rows,)
    rows_spec = pl.BlockSpec((block_rows, model_width), lambda i: (i, 0))
    columns_spec = pl.BlockSpec((block_rows, row_count), lambda i: (i, 0))
    grad_att = call(
        functools.partial(product_kernel, 1, 1), v_wide, blocks,
        [rows_spec, tokens_spec], columns_spec, 0, 0, full_out, grad_branch,
    )
    state_grads, dnum, dden = call(
        state_grad_kernel, (states_low, v_low, head_rows), grid,
        [v_spec, v_spec, row_spec, qk_spec, one_row, table, table, column],
        (state_spec, v_spec, row_spec),
        2 * 10**9, 12 * 10**6,
        grad_att, output, denom, qk, cont, left_low, right_low, query_scale,
    )
    state_grads, result_terms = lax.optimization_barrier((state_grads, result_terms))
    late_attended, state_grads = lax.optimization_barrier((attended, state_grads))
    near_grads = stack_near(state_grads)
    out_terms = call(
        functools.partial(product_kernel, 1, 0),
        jax.ShapeDtypeStruct((v_width, model_width), BF), blocks,
        [columns_spec, tokens_spec], rows_spec, 0, 0, late_attended, grad_branch,
    )
    dnum, out_terms, moved = lax.optimization_barrier((dnum, out_terms, moved))
    queue = SumQueue(orders, [added(k, m) for k, m in zip(kept, moved)])
    grad_queries, dk_local, dv_local = call(
        local_grad_kernel, (qk_low, qk_wide, v_wide), grid,
        [qk_spec, k_spec, v_spec, v_spec, row_spec, square, state_spec, one_row,
         table, table, table_t, table_t, column],
        (qk_spec, qk_spec, v_spec),
        30 * 10**9, 12 * 10**6,
        qk, qk, values, dnum, dden, allowed, state_in, cont,
        left_low, right_low, left_t, right_t, query_scale,
    )
    dk_local, dv_local, near_grads = queue.turn((dk_local, dv_local, near_grads))
    grad_stacks = stack_all(state_grads, near_grads)
    last_result, out_terms, grad_stacks[0] = lax.optimization_barrier(
        (last_result, out_terms, grad_stacks[0])
    )
    result_terms.append(exchanged(last_result, offsets[-1]))
    out_shard = lax.psum_scatter(out_terms, "grp", scatter_dimension=0, tiled=True)
    earlier = sources[None, :] == sources[:, None] - 1
    previous_ids = jnp.sum(jnp.where(earlier, source_ids[None, :], 0.0), axis=1)
    late_marks = ((sources > mine) & (previous_ids == id_float[row_count - 1])).astype(F32)
    grad_keys, grad_values = call(
        functools.partial(late_grad_kernel, len(grad_stacks)), (qk_low, v_low), grid,
        [smem, *map(stack_spec, grad_stacks), k_spec, v_spec, one_row, qk_spec, v_spec,
         table, table, table_t, table_t, column],
        (qk_spec, v_spec),
        2 * 10**9, 14 * 10**6,
        late_marks, *grad_stacks, qk, values, own, dk_local, dv_local,
        left_low, right_low, left_t, right_t, key_scale,
    )
    grad_keys, grad_values = queue.turn((grad_keys, grad_values))
    grad_projected = jnp.concatenate([grad_queries, grad_keys, grad_values], axis=0)
    in_width = full_in.shape[1]
    in_terms = call(
        functools.partial(product_kernel, 0, 1),
        jax.ShapeDtypeStruct((model_width, in_width), BF), (model_width // block_rows,),
        [pl.BlockSpec((row_count, block_rows), lambda i: (0, i)), whole(in_width, row_count)],
        pl.BlockSpec((block_rows, in_width), lambda i: (i, 0)),
        0, 0, mixed, grad_projected,
    )
    grad_projected, result_terms = lax.optimization_barrier((grad_projected, result_terms))
    ffn_result = sum(term.astype(F32) for term in [results[0], *result_terms])
    mixed_out = (residual + ffn_result).astype(BF)
    sum_ffn = jnp.sum(keep_rows * jnp.sum(ffn_result * ffn_result, axis=1))
    mixed_out, sum_ffn, grad_projected = lax.optimization_barrier(
        (mixed_out, sum_ffn, grad_projected)
    )
    in_shard = lax.psum_scatter(in_terms, "grp", scatter_dimension=0, tiled=True)
    grad_mixed = call(
        mixed_grad_kernel, tokens_wide, (model_width // block_rows,),
        [
            whole(in_width, row_count),
            pl.BlockSpec((block_rows, in_width), lambda i: (i, 0)),
        ],
        pl.BlockSpec((row_count, block_rows), lambda i: (0, i)),
        0, 0, grad_projected, full_in,
        scratch=[pltpu.VMEM((row_count, in_width), BF)],
    )
    grad_mixed, out_shard = lax.optimization_barrier((grad_mixed, out_shard))
    out_parts = rep_scattered(out_shard)
    edge_back = jnp.concatenate([grad_mixed[:2] * gated[:2], id_float[:2, None]], axis=1)
    edge_back = passed_along(edge_back, "grp", -1)
    ext_grad_ids = jnp.concatenate([id_float, edge_back[:, model_width]], axis=0)
    ahead_one = (ext_grad_ids[1 : row_count + 1] == id_float).astype(F32)[:, None]
    ahead_two = (ext_grad_ids[2:] == id_float).astype(F32)[:, None]
    flags = jnp.concatenate([same_one, same_two, ahead_one, ahead_two], axis=1)
    grad_tokens, sums = call(
        conv_grad_kernel, (tokens_low, jax.ShapeDtypeStruct((4, model_width), F32)), (1,),
        [
            tokens_spec, whole(2, model_width), whole(2, model_width), whole(row_count, 1),
            whole(row_count, 4), gain_spec, whole(3, model_width), tokens_spec, tokens_spec,
        ],
        (tokens_spec, whole(4, model_width)),
        0, 0,
        tokens, ext_norm[:2], edge_back[:, :model_width], scale_in, flags, norm_gain[None],
        conv_taps.T, grad_mixed, grad_mid,
        scratch=[pltpu.VMEM((row_count, model_width), F32)],
    )

    grad_tokens, sums, out_parts = queue.turn((grad_tokens, sums, out_parts))
    grad_ffn_in, grad_ffn_out = queue.finish()
    in_shard, grad_tokens, sums = lax.optimization_barrier((in_shard, grad_tokens, sums))
    in_parts = rep_scattered(in_shard)

    stat_terms = jnp.stack(
        [
            jnp.sum(keep_rows * jnp.sum(x_full * x_full, axis=1)),
            jnp.sum(keep_rows * jnp.sum(branch * branch, axis=1)),
            sum_ffn,
            jnp.sum(keep_rows),
        ]
    )
    small = jnp.concatenate([sums.reshape(-1), grad_ffn_gain[0], stat_terms])
    small = jnp.pad(small, (0, -small.shape[0] % 1024)).reshape(-1, LANES)
    in_parts, small = lax.optimization_barrier((in_parts, butterfly_sum(small)))
    small = small.reshape(-1)
    grad_mix_in = rep_gathered(sum(p.astype(F32) for p in in_parts).astype(BF))
    grad_mix_out = rep_gathered(sum(p.astype(F32) for p in out_parts).astype(BF))
    rows = small[: 5 * model_width].reshape(5, model_width)
    stats = small[5 * model_width : 5 * model_width + 4]
    layer_stats = jnp.sqrt(stats[:3] / (jnp.maximum(stats[3], 1.0) * model_width))
    return (
        mixed_out,
        grad_tokens,
        rows[0],
        rows[1:4].T,
        grad_mix_in,
        grad_mix_out,
        rows[4],
        grad_ffn_in.astype(F32),
        grad_ffn_out.astype(F32),
        layer_stats,
    )


def solution(mesh):
    split = P(("rep", "grp"), None)
    shard = P("grp", None)
    return jax.shard_map(
        body,
        mesh=mesh,
        in_specs=(
            split, P(("rep", "grp")), P(("rep", "grp")), P(), P(), shard, shard, P(), shard, shard,
            split,
        ),
        out_specs=(split, split, P(), P(), shard, shard, P(), shard, shard, P()),
        check_vma=False,
    )
```
